256 devices in a mesh: lon: 64 (over z, y_hi, x), lat: 4 (over y_lo, core).
Axes of the slice: x: 4, y: 4 (y_hi: 2, y_lo: 2; y = y_hi * 2 + y_lo), z: 8, core: 2. Of those that a mesh axis runs over, the one named last changes fastest.
Arguments:
- saved_states: float32 [4, 12, 2048, 2048], P(None, None, 'lon', 'lat'), may hold values from -2 to 2, as said below
- final_cotangent: float32 [12, 2048, 2048], P(None, 'lon', 'lat'), may hold values from -6 to 6
- gravities: float32 [4], replicated, may hold values from 0.3 to 1.5
- sea_mask: int32 [2048, 2048], P('lon', 'lat'), may hold values 0 or 1
- layer_index: int32 [2048, 2048], P('lon', 'lat'), may hold values from 0 to 3
Outputs:
- initial_gradient: float32 [12, 2048, 2048], P(None, 'lon', 'lat')
- forcing_gradient: float32 [2048, 2048], P('lon', 'lat')
The draws below stay inside these ranges and needn't reach their ends.
Inputs may be any that keep to these rules, and one draw needn't show every extreme that they name: `saved_states`: in each saved state the first 4 channels are layer thicknesses, all positive; the others are velocities.
All inputs are finite; a program needn't handle non-finite values. No bound on the sum of `sea_mask` on one device may be relied on, other than what follows from the above.
Results may differ from the reference program's by a relative error of at most 0.0001.
Values sent between devices are 32-bit elements; how exact they have to be, the bound alone decides.
No kernel may reach another device: no remote copies, remote signals or barrier semaphores. Data moves between devices by JAX's collectives and lax.ppermute only.
A program may use at most 128 MiB of HBM per device.

```python
import math
import jax
import jax.numpy as jnp
from jax import lax

L = 4
STEPS = 4
NLON = 2048
NLAT = 2048


def draw_saved_states(key, part):
    key = jax.random.fold_in(key, 11)
    thick_key = jax.random.fold_in(key, 1)
    flow_key = jax.random.fold_in(key, 2)
    thickness = jax.random.uniform(thick_key, (STEPS, L, NLON, NLAT), jnp.float32, 0.5, 1.5)
    flows = jnp.clip(0.5 * jax.random.normal(flow_key, (STEPS, 2 * L, NLON, NLAT), jnp.float32), -2.0, 2.0)
    return jnp.concatenate([thickness, flows], axis=1).astype(jnp.float32)


def plant(values, key, smallest, high):
    longest = values.shape.index(max(values.shape))
    spots = []
    for shift in (0, 1):
        where = [jax.random.randint(jax.random.fold_in(key, axis), (), 0, length) for axis, length in enumerate(values.shape)]
        where[longest] = (where[longest] + shift) % values.shape[longest]
        spots.append(tuple(where))
    return values.at[spots[0]].set(smallest).at[spots[1]].set(high)


def shard_levels(rng, dims, split, least, high):
    gain, own = 1.0, jax.random.fold_in(rng, 6)
    for dim, blocks in split:
        heights = jnp.exp(jax.random.uniform(jax.random.fold_in(own, dim), (blocks,), jnp.float32, least / len(split), high / len(split)))
        gain = gain * jnp.repeat(heights, dims[dim] // blocks).reshape([-1 if axis == dim else 1 for axis in range(len(dims))])
    return gain


def gaussian(key, extent, width, most, pieces=(), held_as=jnp.bfloat16):
    level = shard_levels(key, extent, pieces, -0.22, 0.18) if pieces else 1.0
    entries = jax.random.normal(key, extent, jnp.float32) * width * level
    return jnp.minimum(jnp.maximum(entries, -most), most).astype(held_as)


def setup_inputs(seed: int = 0) -> dict:
    keys = jax.random.split(jax.random.key(seed), 6)
    saved_states = draw_saved_states(jax.random.fold_in(keys[5], 71), 0)
    final_cotangent = gaussian(keys[1], (3 * L, NLON, NLAT), 1.0, 6.0, ((1, 64), (2, 4)), jnp.float32)
    gravities = jnp.clip(jnp.exp(jax.random.uniform(keys[2], (L,), jnp.float32, math.log(0.3), math.log(1.5))), 0.3, 1.5)
    sea_mask = plant((jax.random.randint(keys[3], (NLON, NLAT), 0, 4) < 3).astype(jnp.int32), jax.random.fold_in(keys[3], 1), 0, 1)
    layer_index = plant(jax.random.randint(keys[4], (NLON, NLAT), 0, L), jax.random.fold_in(keys[4], 1), 0, L - 1).astype(jnp.int32)
    return dict(saved_states=saved_states, final_cotangent=final_cotangent, gravities=gravities, sea_mask=sea_mask, layer_index=layer_index)


TIME_STEP = 0.3
VISCOSITY = 0.1
DIFFUSION = 0.05
BOTTOM_DRAG = 0.2

def gravity_matrix(gravities):
    layer_order = jnp.arange(gravities.shape[0])
    lower_mask = (layer_order[:, None] <= layer_order[None, :]).astype(gravities.dtype)
    weighted = lower_mask * gravities[:, None]
    return jnp.einsum('ik,ij->kj', weighted, lower_mask, precision=lax.Precision.HIGHEST)

def coriolis(lat_rows, total_rows):
    return jnp.sin(jnp.pi * ((lat_rows + 0.5) / total_rows - 0.5))

def centre(field):
    return field[:, 1:-1, 1:-1]

def slope_east(field):
    return 0.5 * (field[:, 2:, 1:-1] - field[:, :-2, 1:-1])

def slope_north(field):
    return 0.5 * (field[:, 1:-1, 2:] - field[:, 1:-1, :-2])

def laplace(field):
    return field[:, 2:, 1:-1] + field[:, :-2, 1:-1] + field[:, 1:-1, 2:] + field[:, 1:-1, :-2] - 4.0 * centre(field)

def advance(state, sea_part, rotation_rate, gravity_table):
    layers = gravity_table.shape[0]
    thickness = state[:layers]
    east_flow = state[layers:2 * layers]
    north_flow = state[2 * layers:]
    montgomery = jnp.einsum('kj,jxy->kxy', gravity_table, thickness, precision=lax.Precision.HIGHEST)
    east_mid = centre(east_flow)
    north_mid = centre(north_flow)
    drag_rate = BOTTOM_DRAG * (jnp.arange(layers) == layers - 1).astype(state.dtype)[:, None, None]
    new_thickness = centre(thickness) - TIME_STEP * (slope_east(thickness * east_flow) + slope_north(thickness * north_flow)) + TIME_STEP * DIFFUSION * laplace(thickness)
    new_east = sea_part * (east_mid + TIME_STEP * (rotation_rate * north_mid - slope_east(montgomery) - east_mid * slope_east(east_flow) - north_mid * slope_north(east_flow) + VISCOSITY * laplace(east_flow) - drag_rate * east_mid))
    new_north = sea_part * (north_mid + TIME_STEP * (-rotation_rate * east_mid - slope_north(montgomery) - east_mid * slope_east(north_flow) - north_mid * slope_north(north_flow) + VISCOSITY * laplace(north_flow) - drag_rate * north_mid))
    return jnp.concatenate([new_thickness, new_east, new_north], axis=0)

def reference(saved_states, final_cotangent, gravities, sea_mask, layer_index):
    gravity_table = gravity_matrix(gravities)
    sea_part = sea_mask.astype(jnp.float32)[None]
    lat_rows = jnp.arange(NLAT).astype(jnp.float32)
    rotation_rate = coriolis(lat_rows, NLAT)[None, None, :]
    chosen = (layer_index[None] == jnp.arange(L, dtype=jnp.int32)[:, None, None]).astype(jnp.float32)

    def forward(state):
        padded = jnp.pad(state, ((0, 0), (1, 1), (0, 0)), mode='wrap')
        padded = jnp.pad(padded, ((0, 0), (0, 0), (1, 1)))
        return advance(padded, sea_part, rotation_rate, gravity_table)
    adjoint = final_cotangent
    forcing = jnp.zeros(sea_mask.shape, jnp.float32)
    for moment in range(STEPS - 1, -1, -1):
        forcing = forcing + TIME_STEP * lax.optimization_barrier(jnp.sum(chosen * adjoint[:L], axis=0))
        _, pullback = jax.vjp(forward, saved_states[moment])
        adjoint, = pullback(adjoint)
    return (adjoint, forcing)
```

```python
import functools

import jax
import jax.numpy as jnp
from jax import lax
from jax.experimental import pallas as pl
from jax.experimental.pallas import tpu as pltpu
from jax.sharding import PartitionSpec as P

TIME_STEP = 0.3
VISCOSITY = 0.1
DIFFUSION = 0.05
BOTTOM_DRAG = 0.2

L = 4
N = 4
CH = 3 * L
ROWS = 32
COLS = 512
RR = ROWS + 2 * N
CC = COLS + 128
T = RR // 8
W = CC // 128


def lanes(j):
    return slice(128 * j, 128 * j + 128)


COT = N * CH
SEA = COT + CH
PLANES = SEA + 1
GROUPS = -(-PLANES // 16)


def depth(q):
    if q >= COT:
        return N
    n, c = divmod(q, CH)
    return n + 1 if c >= L else n


ORDER = sorted(range(PLANES), key=lambda q: -depth(q))
OFFSET = {}
_row = 0
for _q in ORDER:
    if depth(_q):
        OFFSET[_q] = _row
        _row += depth(_q)
HALO_ROWS = _row


def pack_kernel(states, cot, sea, east, west, strips, east_corner, west_corner):
    lane = lax.broadcasted_iota(jnp.int32, (ROWS, 128), 1)

    def plane(q, rows, cols):
        if q == SEA:
            return sea[rows, cols].astype(jnp.float32)
        if q >= COT:
            return cot[q - COT, rows, cols]
        return states[q // CH, q % CH, rows, cols]

    everything = slice(None)
    for q, row in OFFSET.items():
        d = depth(q)
        east[row : row + d] = plane(q, slice(ROWS - d, ROWS), everything)
        west[row : row + d] = plane(q, slice(0, d), everything)
    for g in range(GROUPS):
        total = jnp.zeros((ROWS, 128), jnp.float32)
        for k in range(16):
            q = g * 16 + k
            if q >= PLANES:
                continue
            first = plane(q, everything, slice(0, 128))
            last = plane(q, everything, slice(COLS - 128, COLS))
            both = pltpu.roll(jnp.where(lane >= 124, last, first), (8 * k + 4) % 128, 1)
            total = jnp.where(lane // 8 == k, both, total)
        strips[g] = total
        east_corner[4 * g : 4 * g + 4] = total[ROWS - 4 :]
        west_corner[4 * g : 4 * g + 4] = total[:4]


def step_kernel(
    place,
    gravities,
    states,
    cot,
    sea,
    layer,
    spin,
    from_west,
    from_east,
    from_south,
    from_north,
    sw,
    nw,
    se,
    ne,
    out,
    forcing,
    planes,
    cur,
    nxt,
    mixed,
    acc,
    picked,
    sems,
):
    copies = []
    for n in range(N, -1, -1):
        source = cot if n == N else states.at[n]
        for j in range(W - 1):
            copies.append(
                pltpu.make_async_copy(
                    source.at[:, :, lanes(j)],
                    planes.at[n * CH : (n + 1) * CH, j, :ROWS, :],
                    sems.at[n * W + j],
                )
            )
    for copy in copies:
        copy.start()
    for j in range(W - 1):
        planes[SEA, j, :ROWS, :] = sea[:, lanes(j)].astype(jnp.float32)
        picked[j, :ROWS, :] = layer[:, lanes(j)]

    for q, row in OFFSET.items():
        d = depth(q)
        for j in range(W - 1):
            planes[q, j, ROWS : ROWS + d, :] = from_east[row : row + d, lanes(j)]
            planes[q, j, RR - d : RR, :] = from_west[row : row + d, lanes(j)]
    lane = lax.broadcasted_iota(jnp.int32, (ROWS, 128), 1)
    south_side = lane % 8 < 4
    for g in range(GROUPS):
        edge = jnp.where(south_side, from_south[g], from_north[g])
        rows = slice(4 * g, 4 * g + 4)
        corner = jnp.concatenate(
            [
                jnp.where(south_side[:4], se[rows], ne[rows]),
                jnp.where(south_side[:4], sw[rows], nw[rows]),
            ],
            axis=0,
        )
        for k in range(16):
            q = g * 16 + k
            if q >= PLANES:
                continue
            shift = (128 - (8 * k + 4)) % 128
            planes[q, W - 1, :ROWS, :] = pltpu.roll(edge, shift, 1)
            planes[q, W - 1, ROWS:, :] = pltpu.roll(corner, shift, 1)
    for copy in copies:
        copy.wait()

    def ring(t):
        return pl.ds(t, 8, stride=T)

    def read(q, t):
        return jnp.concatenate([planes[q, j, ring(t), :] for j in range(W)], axis=1)

    def write(q, t, value):
        for j in range(W - 1):
            planes[q, j, ring(t), :] = value[:, lanes(j)]

    for t in range(T):
        sea_t = read(SEA, t)
        for c in range(CH):
            value = read(COT + c, t)
            cur[c, t] = value if c < L else value * sea_t
        acc[t] = jnp.zeros((8, CC), jnp.float32)

    edge_lane = lax.broadcasted_iota(jnp.int32, (8, 128), 1)
    inside = jnp.where(edge_lane < 64, place[0], place[1]) > 0

    def north(x):
        return pltpu.roll(x, CC - 1, 1)

    def south(x):
        return pltpu.roll(x, 1, 1)

    def one_step(index, src, dst):
        n = N - 1 - index

        def east(load, t):
            return load(t + 1) if t + 1 < T else pltpu.roll(load(0), 7, 0)

        def west(load, t):
            return load(t - 1) if t > 0 else pltpu.roll(load(T - 1), 1, 0)

        def layer_body(k, carry):
            load_h = lambda t: read(n * CH + k, t)
            load_u = lambda t: read(n * CH + L + k, t)
            load_v = lambda t: read(n * CH + 2 * L + k, t)
            load_c = lambda t: src[k, t]
            load_p = lambda t: src[L + k, t]
            load_q = lambda t: src[2 * L + k, t]
            half = 0.5 * TIME_STEP
            drag = jnp.where(k == L - 1, BOTTOM_DRAG, 0.0)
            keep = 1.0 - TIME_STEP * (4.0 * VISCOSITY + drag)
            turn = spin[...]
            for t in range(T):
                c, p, q = load_c(t), load_p(t), load_q(t)
                h, u, v = load_h(t), load_u(t), load_v(t)
                ce, cw, cn, cs = east(load_c, t), west(load_c, t), north(c), south(c)
                dcx = ce - cw
                dcy = cn - cs
                pe, pw, pn, ps = east(load_p, t), west(load_p, t), north(p), south(p)
                qe, qw, qn, qs = east(load_q, t), west(load_q, t), north(q), south(q)
                mixed[k, t] = (pe - pw) + (qn - qs)
                dst[k, t] = (1.0 - 4.0 * TIME_STEP * DIFFUSION) * c + half * (
                    u * dcx + v * dcy + (2.0 * DIFFUSION) * ((ce + cw) + (cn + cs))
                )
                ue, uw, un, us = east(load_u, t), west(load_u, t), north(u), south(u)
                ve, vw, vn, vs = east(load_v, t), west(load_v, t), north(v), south(v)
                a_e = ue + 2.0 * VISCOSITY
                a_w = 2.0 * VISCOSITY - uw
                a_n = vn + 2.0 * VISCOSITY
                a_s = 2.0 * VISCOSITY - vs
                new_p = keep * p + half * (
                    h * dcx
                    - turn * q
                    - p * (ue - uw)
                    - q * (ve - vw)
                    + (a_e * pe + a_w * pw)
                    + (a_n * pn + a_s * ps)
                )
                new_q = keep * q + half * (
                    h * dcy
                    + turn * p
                    - p * (un - us)
                    - q * (vn - vs)
                    + (a_e * qe + a_w * qw)
                    + (a_n * qn + a_s * qs)
                )
                mask = jnp.where(n == 0, 1.0, read(SEA, t))
                dst[L + k, t] = new_p * mask
                dst[2 * L + k, t] = new_q * mask
            return carry

        lax.fori_loop(0, L, layer_body, 0)
        half = 0.5 * TIME_STEP
        for t in range(T):
            idx = jnp.concatenate([picked[j, ring(t), :] for j in range(W)], axis=1)
            chosen = jnp.zeros((8, CC), jnp.float32)
            for k in range(L):
                chosen = jnp.where(idx == k, src[k, t], chosen)
            acc[t] = acc[t] + TIME_STEP * chosen
            tails = [None] * L
            total = mixed[L - 1, t]
            tails[L - 1] = total
            for k in range(L - 2, -1, -1):
                total = total + mixed[k, t]
                tails[k] = total
            head = None
            for k in range(L):
                term = (half * gravities[k]) * tails[k]
                head = term if head is None else head + term
                new = dst[k, t] + head
                dst[k, t, :, :COLS] = new[:, :COLS]
                dst[k, t, :, COLS:] = jnp.where(inside, new[:, COLS:], 0.0)

    def two_steps(i, carry):
        one_step(2 * i, cur, nxt)
        one_step(2 * i + 1, nxt, cur)
        return carry

    lax.fori_loop(0, N // 2, two_steps, 0)

    for t in range(T):
        for c in range(CH):
            write(COT + c, t, cur[c, t])
        write(SEA, t, acc[t])
    final = []
    for j in range(W - 1):
        final.append(
            pltpu.make_async_copy(planes.at[COT : COT + CH, j, :ROWS, :], out.at[:, :, lanes(j)], sems.at[2 * j])
        )
        final.append(pltpu.make_async_copy(planes.at[SEA, j, :ROWS, :], forcing.at[:, lanes(j)], sems.at[2 * j + 1]))
    for copy in final:
        copy.start()
    for copy in final:
        copy.wait()


VMEM = pl.BlockSpec(memory_space=pltpu.VMEM)
SMEM = pl.BlockSpec(memory_space=pltpu.SMEM)
ANY = pl.BlockSpec(memory_space=pl.ANY)
f32 = jnp.float32


def per_device(saved_states, final_cotangent, gravities, sea_mask, layer_index):
    lons, lats = lax.axis_size("lon"), lax.axis_size("lat")
    lat = lax.axis_index("lat")
    lane = jnp.arange(CC, dtype=jnp.int32)
    lane = jnp.where(lane < COLS + 64, lane, lane - CC)
    lat_rows = (lat * COLS + lane).astype(f32)
    spin = 2.0 * jnp.sin(jnp.pi * ((lat_rows + 0.5) / (lats * COLS) - 0.5))
    spin = jnp.broadcast_to(spin[None], (8, CC))
    place = jnp.stack([(lat < lats - 1).astype(jnp.int32), (lat > 0).astype(jnp.int32)])

    shape = jax.ShapeDtypeStruct
    east, west, strips, east_corner, west_corner = pl.pallas_call(
        pack_kernel,
        out_shape=[
            shape((HALO_ROWS, COLS), f32),
            shape((HALO_ROWS, COLS), f32),
            shape((GROUPS, ROWS, 128), f32),
            shape((4 * GROUPS, 128), f32),
            shape((4 * GROUPS, 128), f32),
        ],
        in_specs=[VMEM] * 3,
        out_specs=[VMEM] * 5,
        compiler_params=pltpu.CompilerParams(vmem_limit_bytes=24 << 20),
    )(saved_states, final_cotangent, sea_mask)

    def send(x, dx, dy):
        pairs = []
        for i in range(lons):
            for j in range(lats):
                if 0 <= j + dy < lats:
                    pairs.append((i * lats + j, ((i + dx) % lons) * lats + j + dy))
        return lax.ppermute(x, ("lon", "lat"), pairs)

    from_west = send(east, 1, 0)
    sw = send(east_corner, 1, 1)
    nw = send(east_corner, 1, -1)
    from_east = send(west, -1, 0)
    se = send(west_corner, -1, 1)
    ne = send(west_corner, -1, -1)
    from_south = send(strips, 0, 1)
    from_north = send(strips, 0, -1)

    return pl.pallas_call(
        step_kernel,
        out_shape=[shape((CH, ROWS, COLS), f32), shape((ROWS, COLS), f32)],
        in_specs=[SMEM, SMEM, ANY, ANY] + [VMEM] * 11,
        out_specs=[ANY, ANY],
        scratch_shapes=[
            pltpu.VMEM((PLANES, W, RR, 128), f32),
            pltpu.VMEM((CH, T, 8, CC), f32),
            pltpu.VMEM((CH, T, 8, CC), f32),
            pltpu.VMEM((L, T, 8, CC), f32),
            pltpu.VMEM((T, 8, CC), f32),
            pltpu.VMEM((W, RR, 128), jnp.int32),
            pltpu.SemaphoreType.DMA(((N + 1) * W,)),
        ],
        compiler_params=pltpu.CompilerParams(vmem_limit_bytes=40 << 20),
    )(
        place,
        gravities,
        saved_states,
        final_cotangent,
        sea_mask,
        layer_index,
        spin,
        from_west,
        from_east,
        from_south,
        from_north,
        sw,
        nw,
        se,
        ne,
    )


def solution(mesh):
    return jax.shard_map(
        per_device,
        mesh=mesh,
        in_specs=(
            P(None, None, "lon", "lat"),
            P(None, "lon", "lat"),
            P(),
            P("lon", "lat"),
            P("lon", "lat"),
        ),
        out_specs=(P(None, "lon", "lat"), P("lon", "lat")),
        check_vma=False,
    )
```

```python
import jax
import jax.numpy as jnp
from jax import lax
from jax.experimental import pallas as pl
from jax.experimental.pallas import tpu as pltpu
from jax.sharding import PartitionSpec as P

TIME_STEP = 0.3
VISCOSITY = 0.1
DIFFUSION = 0.05
BOTTOM_DRAG = 0.2

L = 4
N = 4
CH = 3 * L
ROWS = 32
COLS = 512
CC = COLS + 128
W = CC // 128
RIM = 16 + 2 * N

COT = N * CH
SEA = COT + CH
PLANES = SEA + 1
GROUPS = -(-PLANES // 16)
f32 = jnp.float32


def lanes(j):
    return slice(128 * j, 128 * j + 128)


def depth(q):
    if q >= COT:
        return N
    n, c = divmod(q, CH)
    return n + 1 if c >= L else n


OFFSET = {}
HALO = 0
for _q in sorted(range(PLANES), key=lambda q: -depth(q)):
    if depth(_q):
        OFFSET[_q] = HALO
        HALO += depth(_q)
MESSAGE = HALO + N


def start(pairs, sems):
    copies = [pltpu.make_async_copy(a, b, sems.at[i]) for i, (a, b) in enumerate(pairs)]
    for copy in copies:
        copy.start()
    return copies


def wait(copies):
    for copy in copies:
        copy.wait()


def strip_pack_kernel(states, cot, sea, strips, left, right, flags, sems):
    pairs = [(sea, flags)]
    for buf, cols in ((left, slice(0, 128)), (right, slice(COLS - 128, COLS))):
        pairs.append((states.at[:, :, :, cols], buf.at[:N]))
        pairs.append((cot.at[:, :, cols], buf.at[N]))
    wait(start(pairs, sems))
    lane = lax.broadcasted_iota(jnp.int32, (ROWS, 128), 1)
    for g in range(GROUPS):
        total = jnp.zeros((ROWS, 128), f32)
        for k in range(16):
            q = g * 16 + k
            if q >= PLANES:
                continue
            if q == SEA:
                first, last = flags[:, lanes(0)].astype(f32), flags[:, lanes(W - 2)].astype(f32)
            else:
                first, last = left[q // CH, q % CH], right[q // CH, q % CH]
            both = pltpu.roll(jnp.where(lane >= 124, last, first), (8 * k + 4) % 128, 1)
            total = jnp.where(lane // 8 == k, both, total)
        strips[g] = total


def row_pack_kernel(place, states, cot, sea, pair, middle, east, west, edge, top, bottom, flags, sems):
    pairs = [(sea, flags)]
    for buf, rows in ((top, slice(0, 8)), (bottom, slice(ROWS - 8, ROWS))):
        pairs.append((states.at[:, :, rows, :], buf.at[:N]))
        pairs.append((cot.at[:, rows, :], buf.at[N]))
    copies = start(pairs, sems)
    south = lax.broadcasted_iota(jnp.int32, (ROWS, 128), 1) % 8 < 4
    for g in range(GROUPS):
        merged = jnp.where(south == (place[0] == 1), pair[g], middle[g])
        edge[g] = merged
        east[HALO:, lanes(g)] = merged[ROWS - N :]
        west[HALO:, lanes(g)] = merged[:N]
    wait(copies)
    for q, row in OFFSET.items():
        d = depth(q)
        if q == SEA:
            east[row : row + d] = flags[ROWS - d :].astype(f32)
            west[row : row + d] = flags[:d].astype(f32)
        else:
            east[row : row + d] = bottom[q // CH, q % CH, 8 - d :]
            west[row : row + d] = top[q // CH, q % CH, :d]


def fill_halo(planes, message, first, last):
    for q, row in OFFSET.items():
        d = depth(q)
        at = first if last is None else last - d
        for j in range(W - 1):
            planes[q, j, at : at + d, :] = message[row : row + d, lanes(j)]
    at = first if last is None else last - N
    for q in range(PLANES):
        g, k = divmod(q, 16)
        planes[q, W - 1, at : at + N, :] = pltpu.roll(message[HALO:, lanes(g)], (124 - 8 * k) % 128, 1)


def fill_columns(planes, edge, blocks):
    for source, target, count in blocks:
        for q in range(PLANES):
            g, k = divmod(q, 16)
            planes[q, W - 1, target : target + count, :] = pltpu.roll(
                edge[g, source : source + count, :], (124 - 8 * k) % 128, 1
            )


def own_copies(n, source, planes, blocks, sems):
    return [
        pltpu.make_async_copy(
            source.at[:, row : row + count, lanes(j)],
            planes.at[pl.ds(n * CH, CH), j, target : target + count, :],
            sems.at[n, j, i],
        )
        for i, (row, target, count) in enumerate(blocks)
        for j in range(W - 1)
    ]


def adjoint_steps(rows, arrive, place, gravities, spin, planes, picked, cur, nxt, mixed, acc):
    T = rows // 8
    half = 0.5 * TIME_STEP

    def ring(t):
        return pl.ds(t, 8, stride=T)

    def read(q, t):
        return jnp.concatenate([planes[q, j, ring(t), :] for j in range(W)], axis=1)

    def write(q, t, value):
        for j in range(W - 1):
            planes[q, j, ring(t), :] = value[:, lanes(j)]

    for t in range(T):
        sea_t = read(SEA, t)
        for c in range(CH):
            value = read(COT + c, t)
            cur[c, t] = value if c < L else value * sea_t
        acc[t] = jnp.zeros((8, CC), f32)

    edge_lane = lax.broadcasted_iota(jnp.int32, (8, 128), 1)
    inside = jnp.where(edge_lane < 64, place[1], place[2]) > 0

    def north(x):
        return pltpu.roll(x, CC - 1, 1)

    def south(x):
        return pltpu.roll(x, 1, 1)

    def east(load, t):
        return load(t + 1) if t + 1 < T else pltpu.roll(load(0), 7, 0)

    def west(load, t):
        return load(t - 1) if t > 0 else pltpu.roll(load(T - 1), 1, 0)

    def one_step(index, src, dst):
        n = N - 1 - index
        arrive(n)

        def layer_body(k, carry):
            load_h = lambda t: read(n * CH + k, t)
            load_u = lambda t: read(n * CH + L + k, t)
            load_v = lambda t: read(n * CH + 2 * L + k, t)
            load_c = lambda t: src[k, t]
            load_p = lambda t: src[L + k, t]
            load_q = lambda t: src[2 * L + k, t]
            drag = jnp.where(k == L - 1, BOTTOM_DRAG, 0.0)
            keep = 1.0 - TIME_STEP * (4.0 * VISCOSITY + drag)
            turn = spin[...]
            for t in range(T):
                c, p, q = load_c(t), load_p(t), load_q(t)
                h, u, v = load_h(t), load_u(t), load_v(t)
                ce, cw, cn, cs = east(load_c, t), west(load_c, t), north(c), south(c)
                dcx = ce - cw
                dcy = cn - cs
                pe, pw, pn, ps = east(load_p, t), west(load_p, t), north(p), south(p)
                qe, qw, qn, qs = east(load_q, t), west(load_q, t), north(q), south(q)
                mixed[k, t] = (pe - pw) + (qn - qs)
                dst[k, t] = (1.0 - 4.0 * TIME_STEP * DIFFUSION) * c + half * (
                    u * dcx + v * dcy + (2.0 * DIFFUSION) * ((ce + cw) + (cn + cs))
                )
                ue, uw, un, us = east(load_u, t), west(load_u, t), north(u), south(u)
                ve, vw, vn, vs = east(load_v, t), west(load_v, t), north(v), south(v)
                a_e = ue + 2.0 * VISCOSITY
                a_w = 2.0 * VISCOSITY - uw
                a_n = vn + 2.0 * VISCOSITY
                a_s = 2.0 * VISCOSITY - vs
                new_p = keep * p + half * (
                    h * dcx
                    - turn * q
                    - p * (ue - uw)
                    - q * (ve - vw)
                    + (a_e * pe + a_w * pw)
                    + (a_n * pn + a_s * ps)
                )
                new_q = keep * q + half * (
                    h * dcy
                    + turn * p
                    - p * (un - us)
                    - q * (vn - vs)
                    + (a_e * qe + a_w * qw)
                    + (a_n * qn + a_s * qs)
                )
                mask = jnp.where(n == 0, 1.0, read(SEA, t))
                dst[L + k, t] = new_p * mask
                dst[2 * L + k, t] = new_q * mask
            return carry

        lax.fori_loop(0, L, layer_body, 0)
        for t in range(T):
            idx = jnp.concatenate([picked[j, ring(t), :] for j in range(W)], axis=1)
            chosen = jnp.zeros((8, CC), f32)
            for k in range(L):
                chosen = jnp.where(idx == k, src[k, t], chosen)
            acc[t] = acc[t] + TIME_STEP * chosen
            total = mixed[L - 1, t]
            tails = [total]
            for k in range(L - 2, -1, -1):
                total = total + mixed[k, t]
                tails.insert(0, total)
            head = None
            for k in range(L):
                term = (half * gravities[k]) * tails[k]
                head = term if head is None else head + term
                new = dst[k, t] + head
                dst[k, t, :, :COLS] = new[:, :COLS]
                dst[k, t, :, COLS:] = jnp.where(inside, new[:, COLS:], 0.0)

    def two_steps(i, carry):
        one_step(2 * i, cur, nxt)
        one_step(2 * i + 1, nxt, cur)
        return carry

    lax.fori_loop(0, N // 2, two_steps, 0)

    for t in range(T):
        for c in range(CH):
            write(COT + c, t, cur[c, t])
        write(SEA, t, acc[t])


def layer_copies(layer, picked, blocks):
    return [
        (layer.at[row : row + count, lanes(j)], picked.at[j, target : target + count, :])
        for row, target, count in blocks
        for j in range(W - 1)
    ]


def main_kernel(
    place,
    gravities,
    states,
    cot,
    sea,
    layer,
    spin,
    edge,
    out,
    forcing,
    planes,
    cur,
    nxt,
    mixed,
    acc,
    picked,
    flags,
    spins,
    edges,
    sems,
    more,
):
    blocks = [(0, 0, ROWS)]
    first = start([(sea, flags), (edge, edges), (spin, spins)] + layer_copies(layer, picked, blocks), more)
    copies = [own_copies(N, cot, planes, blocks, sems)]
    for n in range(N - 1, -1, -1):
        copies.append(own_copies(n, states.at[n], planes, blocks, sems))
    for group in copies:
        for copy in group:
            copy.start()
    wait(first)
    for j in range(W - 1):
        planes[SEA, j, :ROWS, :] = flags[:, lanes(j)].astype(f32)
    fill_columns(planes, edges, blocks)
    wait(copies[0])
    adjoint_steps(
        ROWS,
        lambda n: wait(own_copies(n, states.at[n], planes, blocks, sems)),
        place,
        gravities,
        spins,
        planes,
        picked,
        cur,
        nxt,
        mixed,
        acc,
    )
    pairs = []
    for j in range(W - 1):
        pairs.append((planes.at[COT : COT + CH, j, :ROWS, :], out.at[:, :, lanes(j)]))
        pairs.append((planes.at[SEA, j, :ROWS, :], forcing.at[:, lanes(j)]))
    wait(start(pairs, more))


def rim_kernel(
    place,
    gravities,
    states,
    cot,
    sea,
    layer,
    spin,
    from_west,
    from_east,
    edge,
    out_in,
    forcing_in,
    out,
    forcing,
    planes,
    cur,
    nxt,
    mixed,
    acc,
    picked,
    flags,
    spins,
    edges,
    wests,
    easts,
    tiles,
    sems,
    more,
):
    blocks = [(ROWS - 8, 0, 8), (0, RIM - 8, 8)]
    late = start([(from_west, wests), (from_east, easts)], more.at[:2])
    first = start([(sea, flags), (edge, edges), (spin, spins)] + layer_copies(layer, picked, blocks), more.at[2:])
    copies = [own_copies(N, cot, planes, blocks, sems)]
    for n in range(N - 1, -1, -1):
        copies.append(own_copies(n, states.at[n], planes, blocks, sems))
    for group in copies:
        for copy in group:
            copy.start()
    back = []
    for i, (row, _, _) in enumerate(blocks):
        back.append((out_in.at[:, row : row + 8, :], tiles.at[i, :CH]))
        back.append((forcing_in.at[row : row + 8, :], tiles.at[i, CH]))
    back = start(back, more.at[13:])
    wait(first)
    for row, target, _ in blocks:
        for j in range(W - 1):
            planes[SEA, j, target : target + 8, :] = flags[row : row + 8, lanes(j)].astype(f32)
    fill_columns(planes, edges, blocks)
    wait(late)
    fill_halo(planes, easts, 8, None)
    fill_halo(planes, wests, None, RIM - 8)
    wait(copies[0])
    adjoint_steps(
        RIM,
        lambda n: wait(own_copies(n, states.at[n], planes, blocks, sems)),
        place,
        gravities,
        spins,
        planes,
        picked,
        cur,
        nxt,
        mixed,
        acc,
    )
    wait(back)
    sublane = lax.broadcasted_iota(jnp.int32, (8, 128), 0)
    pairs = []
    for i, (row, target, _) in enumerate(blocks):
        late_row = sublane >= N if row else sublane < N
        for c in range(CH + 1):
            for j in range(W - 1):
                tiles[i, c, :, lanes(j)] = jnp.where(
                    late_row, planes[COT + c, j, target : target + 8, :], tiles[i, c, :, lanes(j)]
                )
        pairs.append((tiles.at[i, :CH], out.at[:, row : row + 8, :]))
        pairs.append((tiles.at[i, CH], forcing.at[row : row + 8, :]))
    wait(start(pairs, more))


VMEM = pl.BlockSpec(memory_space=pltpu.VMEM)
SMEM = pl.BlockSpec(memory_space=pltpu.SMEM)
ANY = pl.BlockSpec(memory_space=pl.ANY)
HBM = pl.BlockSpec(memory_space=pltpu.HBM)
DMA = pltpu.SemaphoreType.DMA
shape = jax.ShapeDtypeStruct


def ring_scratch(rows):
    T = rows // 8
    return [
        pltpu.VMEM((PLANES, W, rows, 128), f32),
        pltpu.VMEM((CH, T, 8, CC), f32),
        pltpu.VMEM((CH, T, 8, CC), f32),
        pltpu.VMEM((L, T, 8, CC), f32),
        pltpu.VMEM((T, 8, CC), f32),
        pltpu.VMEM((W, rows, 128), jnp.int32),
        pltpu.VMEM((ROWS, COLS), jnp.int32),
        pltpu.VMEM((8, CC), f32),
        pltpu.VMEM((GROUPS, ROWS, 128), f32),
    ]


def per_device(saved_states, final_cotangent, gravities, sea_mask, layer_index):
    lons, lats = lax.axis_size("lon"), lax.axis_size("lat")
    lat = lax.axis_index("lat")
    lane = jnp.arange(CC, dtype=jnp.int32)
    lane = jnp.where(lane < COLS + 64, lane, lane - CC)
    lat_rows = (lat * COLS + lane).astype(f32)
    spin = 2.0 * jnp.sin(jnp.pi * ((lat_rows + 0.5) / (lats * COLS) - 0.5))
    spin = jnp.broadcast_to(spin[None], (8, CC))
    place = jnp.stack([lat % 2, (lat < lats - 1).astype(jnp.int32), (lat > 0).astype(jnp.int32)])

    strips = pl.pallas_call(
        strip_pack_kernel,
        out_shape=shape((GROUPS, ROWS, 128), f32),
        in_specs=[HBM] * 3,
        out_specs=VMEM,
        scratch_shapes=[
            pltpu.VMEM((N + 1, CH, ROWS, 128), f32),
            pltpu.VMEM((N + 1, CH, ROWS, 128), f32),
            pltpu.VMEM((ROWS, COLS), jnp.int32),
            DMA((5,)),
        ],
        compiler_params=pltpu.CompilerParams(vmem_limit_bytes=60 << 20),
    )(saved_states, final_cotangent, sea_mask)

    def at(i, j):
        return (i % lons) * lats + j

    def swap(x, first):
        pairs = [(at(i, j), at(i, j + 1)) for i in range(lons) for j in range(first, lats - 1, 2)]
        return lax.ppermute(x, ("lon", "lat"), pairs + [(b, a) for a, b in pairs])

    def shift(x, by):
        return lax.ppermute(x, "lon", [(i, (i + by) % lons) for i in range(lons)])

    pair, middle = swap(strips, 0), swap(strips, 1)
    east, west, edge = pl.pallas_call(
        row_pack_kernel,
        out_shape=[shape((MESSAGE, COLS), f32), shape((MESSAGE, COLS), f32), shape((GROUPS, ROWS, 128), f32)],
        in_specs=[SMEM, HBM, HBM, HBM, VMEM, VMEM],
        out_specs=[VMEM] * 3,
        scratch_shapes=[
            pltpu.VMEM((N + 1, CH, 8, COLS), f32),
            pltpu.VMEM((N + 1, CH, 8, COLS), f32),
            pltpu.VMEM((ROWS, COLS), jnp.int32),
            DMA((5,)),
        ],
        compiler_params=pltpu.CompilerParams(vmem_limit_bytes=53 << 20),
    )(place, saved_states, final_cotangent, sea_mask, pair, middle)
    from_west, from_east = shift(east, 1), shift(west, -1)

    outs = [shape((CH, ROWS, COLS), f32), shape((ROWS, COLS), f32)]
    out, forcing = pl.pallas_call(
        main_kernel,
        out_shape=outs,
        in_specs=[SMEM, SMEM] + [HBM] * 4 + [ANY] * 2,
        out_specs=[HBM, HBM],
        scratch_shapes=ring_scratch(ROWS) + [DMA((N + 1, W - 1, 1)), DMA((16,))],
        compiler_params=pltpu.CompilerParams(vmem_limit_bytes=53 << 20),
        cost_estimate=pl.CostEstimate(flops=160_000_000, bytes_accessed=24_000_000, transcendentals=0),
    )(place, gravities, saved_states, final_cotangent, sea_mask, layer_index, spin, edge)

    return pl.pallas_call(
        rim_kernel,
        out_shape=outs,
        in_specs=[SMEM, SMEM] + [HBM] * 4 + [ANY] * 4 + [HBM] * 2,
        out_specs=[HBM, HBM],
        scratch_shapes=ring_scratch(RIM)
        + [
            pltpu.VMEM((MESSAGE, COLS), f32),
            pltpu.VMEM((MESSAGE, COLS), f32),
            pltpu.VMEM((2, CH + 1, 8, COLS), f32),
            DMA((N + 1, W - 1, 2)),
            DMA((20,)),
        ],
        input_output_aliases={10: 0, 11: 1},
        compiler_params=pltpu.CompilerParams(vmem_limit_bytes=53 << 20),
    )(
        place,
        gravities,
        saved_states,
        final_cotangent,
        sea_mask,
        layer_index,
        spin,
        from_west,
        from_east,
        edge,
        out,
        forcing,
    )


def solution(mesh):
    return jax.shard_map(
        per_device,
        mesh=mesh,
        in_specs=(
            P(None, None, "lon", "lat"),
            P(None, "lon", "lat"),
            P(),
            P("lon", "lat"),
            P("lon", "lat"),
        ),
        out_specs=(P(None, "lon", "lat"), P("lon", "lat")),
        check_vma=False,
    )
```

```python
import jax
import jax.numpy as jnp
from jax import lax
from jax.experimental import pallas as pl
from jax.experimental.pallas import tpu as pltpu
from jax.sharding import PartitionSpec as P

TIME_STEP = 0.3
VISCOSITY = 0.1
DIFFUSION = 0.05
BOTTOM_DRAG = 0.2

L = 4
N = 4
CH = 3 * L
ROWS = 32
COLS = 512
CC = COLS + 128
W = CC // 128

COT = N * CH
SEA = COT + CH
PLANES = SEA + 1
GROUPS = -(-PLANES // 16)
f32 = jnp.float32


def lanes(j):
    return slice(128 * j, 128 * j + 128)


def depth(q):
    if q >= COT:
        return N
    n, c = divmod(q, CH)
    return n + 1 if c >= L else n


OFFSET = {}
HALO = 0
for _q in sorted(range(PLANES), key=lambda q: -depth(q)):
    if depth(_q):
        OFFSET[_q] = HALO
        HALO += depth(_q)
MESSAGE = HALO + N


def start(pairs, sems):
    copies = [pltpu.make_async_copy(a, b, sems.at[i]) for i, (a, b) in enumerate(pairs)]
    for copy in copies:
        copy.start()
    return copies


def wait(copies):
    for copy in copies:
        copy.wait()


def strip_pack_kernel(states, cot, sea, strips, left, right, flags, sems):
    pairs = [(sea, flags)]
    for buf, cols in ((left, slice(0, 128)), (right, slice(COLS - 128, COLS))):
        pairs.append((states.at[:, :, :, cols], buf.at[:N]))
        pairs.append((cot.at[:, :, cols], buf.at[N]))
    wait(start(pairs, sems))
    lane = lax.broadcasted_iota(jnp.int32, (ROWS, 128), 1)
    for g in range(GROUPS):
        total = jnp.zeros((ROWS, 128), f32)
        for k in range(16):
            q = g * 16 + k
            if q >= PLANES:
                continue
            if q == SEA:
                first, last = flags[:, lanes(0)].astype(f32), flags[:, lanes(W - 2)].astype(f32)
            else:
                first, last = left[q // CH, q % CH], right[q // CH, q % CH]
            both = pltpu.roll(jnp.where(lane >= 124, last, first), (8 * k + 4) % 128, 1)
            total = jnp.where(lane // 8 == k, both, total)
        strips[g] = total


def row_pack_kernel(place, states, cot, sea, pair, middle, east, west, edge, top, bottom, flags, sems):
    pairs = [(sea, flags)]
    for buf, rows in ((top, slice(0, 8)), (bottom, slice(ROWS - 8, ROWS))):
        pairs.append((states.at[:, :, rows, :], buf.at[:N]))
        pairs.append((cot.at[:, rows, :], buf.at[N]))
    copies = start(pairs, sems)
    south = lax.broadcasted_iota(jnp.int32, (ROWS, 128), 1) % 8 < 4
    for g in range(GROUPS):
        merged = jnp.where(south == (place[0] == 1), pair[g], middle[g])
        edge[g] = merged
        east[HALO:, lanes(g)] = merged[ROWS - N :]
        west[HALO:, lanes(g)] = merged[:N]
    wait(copies)
    for q, row in OFFSET.items():
        d = depth(q)
        if q == SEA:
            east[row : row + d] = flags[ROWS - d :].astype(f32)
            west[row : row + d] = flags[:d].astype(f32)
        else:
            east[row : row + d] = bottom[q // CH, q % CH, 8 - d :]
            west[row : row + d] = top[q // CH, q % CH, :d]


def fill_halo(planes, message, first, last):
    for q, row in OFFSET.items():
        d = depth(q)
        at = first if last is None else last - d
        for j in range(W - 1):
            planes[q, j, at : at + d, :] = message[row : row + d, lanes(j)]
    at = first if last is None else last - N
    for q in range(PLANES):
        g, k = divmod(q, 16)
        planes[q, W - 1, at : at + N, :] = pltpu.roll(message[HALO:, lanes(g)], (124 - 8 * k) % 128, 1)


def fill_columns(planes, edge, blocks):
    for source, target, count in blocks:
        for q in range(PLANES):
            g, k = divmod(q, 16)
            planes[q, W - 1, target : target + count, :] = pltpu.roll(
                edge[g, source : source + count, :], (124 - 8 * k) % 128, 1
            )


def own_copies(n, source, planes, blocks, sems):
    return [
        pltpu.make_async_copy(
            source.at[:, row : row + count, lanes(j)],
            planes.at[pl.ds(n * CH, CH), j, target : target + count, :],
            sems.at[n, j, i],
        )
        for i, (row, target, count) in enumerate(blocks)
        for j in range(W - 1)
    ]


def adjoint_steps(rows, arrive, place, gravities, spin, planes, picked, cur, nxt, mixed, acc):
    T = rows // 8
    half = 0.5 * TIME_STEP

    def ring(t):
        return pl.ds(t, 8, stride=T)

    def read(q, t):
        return jnp.concatenate([planes[q, j, ring(t), :] for j in range(W)], axis=1)

    def write(q, t, value):
        for j in range(W - 1):
            planes[q, j, ring(t), :] = value[:, lanes(j)]

    for t in range(T):
        sea_t = read(SEA, t)
        for c in range(CH):
            value = read(COT + c, t)
            cur[c, t] = value if c < L else value * sea_t
        acc[t] = jnp.zeros((8, CC), f32)

    edge_lane = lax.broadcasted_iota(jnp.int32, (8, 128), 1)
    inside = jnp.where(edge_lane < 64, place[1], place[2]) > 0

    def north(x):
        return pltpu.roll(x, CC - 1, 1)

    def south(x):
        return pltpu.roll(x, 1, 1)

    def east(load, t):
        return load(t + 1) if t + 1 < T else pltpu.roll(load(0), 7, 0)

    def west(load, t):
        return load(t - 1) if t > 0 else pltpu.roll(load(T - 1), 1, 0)

    def one_step(index, src, dst):
        n = N - 1 - index
        arrive(n)

        def layer_body(k, carry):
            load_h = lambda t: read(n * CH + k, t)
            load_u = lambda t: read(n * CH + L + k, t)
            load_v = lambda t: read(n * CH + 2 * L + k, t)
            load_c = lambda t: src[k, t]
            load_p = lambda t: src[L + k, t]
            load_q = lambda t: src[2 * L + k, t]
            drag = jnp.where(k == L - 1, BOTTOM_DRAG, 0.0)
            keep = 1.0 - TIME_STEP * (4.0 * VISCOSITY + drag)
            turn = spin[...]
            for t in range(T):
                c, p, q = load_c(t), load_p(t), load_q(t)
                h, u, v = load_h(t), load_u(t), load_v(t)
                ce, cw, cn, cs = east(load_c, t), west(load_c, t), north(c), south(c)
                dcx = ce - cw
                dcy = cn - cs
                pe, pw, pn, ps = east(load_p, t), west(load_p, t), north(p), south(p)
                qe, qw, qn, qs = east(load_q, t), west(load_q, t), north(q), south(q)
                mixed[k, t] = (pe - pw) + (qn - qs)
                dst[k, t] = (1.0 - 4.0 * TIME_STEP * DIFFUSION) * c + half * (
                    u * dcx + v * dcy + (2.0 * DIFFUSION) * ((ce + cw) + (cn + cs))
                )
                ue, uw, un, us = east(load_u, t), west(load_u, t), north(u), south(u)
                ve, vw, vn, vs = east(load_v, t), west(load_v, t), north(v), south(v)
                a_e = ue + 2.0 * VISCOSITY
                a_w = 2.0 * VISCOSITY - uw
                a_n = vn + 2.0 * VISCOSITY
                a_s = 2.0 * VISCOSITY - vs
                new_p = keep * p + half * (
                    h * dcx
                    - turn * q
                    - p * (ue - uw)
                    - q * (ve - vw)
                    + (a_e * pe + a_w * pw)
                    + (a_n * pn + a_s * ps)
                )
                new_q = keep * q + half * (
                    h * dcy
                    + turn * p
                    - p * (un - us)
                    - q * (vn - vs)
                    + (a_e * qe + a_w * qw)
                    + (a_n * qn + a_s * qs)
                )
                mask = jnp.where(n == 0, 1.0, read(SEA, t))
                dst[L + k, t] = new_p * mask
                dst[2 * L + k, t] = new_q * mask
            return carry

        lax.fori_loop(0, L, layer_body, 0)
        for t in range(T):
            idx = jnp.concatenate([picked[j, ring(t), :] for j in range(W)], axis=1)
            chosen = jnp.zeros((8, CC), f32)
            for k in range(L):
                chosen = jnp.where(idx == k, src[k, t], chosen)
            acc[t] = acc[t] + TIME_STEP * chosen
            total = mixed[L - 1, t]
            tails = [total]
            for k in range(L - 2, -1, -1):
                total = total + mixed[k, t]
                tails.insert(0, total)
            head = None
            for k in range(L):
                term = (half * gravities[k]) * tails[k]
                head = term if head is None else head + term
                new = dst[k, t] + head
                dst[k, t, :, :COLS] = new[:, :COLS]
                dst[k, t, :, COLS:] = jnp.where(inside, new[:, COLS:], 0.0)

    def two_steps(i, carry):
        one_step(2 * i, cur, nxt)
        one_step(2 * i + 1, nxt, cur)
        return carry

    lax.fori_loop(0, N // 2, two_steps, 0)

    for t in range(T):
        for c in range(CH):
            write(COT + c, t, cur[c, t])
        write(SEA, t, acc[t])


def layer_copies(layer, picked, blocks):
    return [
        (layer.at[row : row + count, lanes(j)], picked.at[j, target : target + count, :])
        for row, target, count in blocks
        for j in range(W - 1)
    ]


def main_kernel(
    place,
    gravities,
    states,
    cot,
    sea,
    layer,
    spin,
    edge,
    out,
    forcing,
    planes,
    cur,
    nxt,
    mixed,
    acc,
    picked,
    flags,
    spins,
    edges,
    sems,
    more,
):
    blocks = [(0, 0, ROWS)]
    first = start([(sea, flags), (edge, edges), (spin, spins)] + layer_copies(layer, picked, blocks), more)
    copies = [own_copies(N, cot, planes, blocks, sems)]
    for n in range(N - 1, -1, -1):
        copies.append(own_copies(n, states.at[n], planes, blocks, sems))
    for group in copies:
        for copy in group:
            copy.start()
    wait(first)
    for j in range(W - 1):
        planes[SEA, j, :ROWS, :] = flags[:, lanes(j)].astype(f32)
    fill_columns(planes, edges, blocks)
    wait(copies[0])
    adjoint_steps(
        ROWS,
        lambda n: wait(own_copies(n, states.at[n], planes, blocks, sems)),
        place,
        gravities,
        spins,
        planes,
        picked,
        cur,
        nxt,
        mixed,
        acc,
    )
    pairs = []
    for j in range(W - 1):
        pairs.append((planes.at[COT : COT + CH, j, :ROWS, :], out.at[:, :, lanes(j)]))
        pairs.append((planes.at[SEA, j, :ROWS, :], forcing.at[:, lanes(j)]))
    wait(start(pairs, more))


def rim_kernel(
    place,
    gravities,
    states,
    cot,
    sea,
    layer,
    spin,
    from_west,
    from_east,
    edge,
    out_in,
    forcing_in,
    out,
    forcing,
    own,
    fields,
    cur,
    nxt,
    mask,
    acc,
    picked,
    flags,
    layers,
    spins,
    edges,
    wests,
    easts,
    tiles,
    sems,
    more,
):
    first = start([(from_west, wests), (from_east, easts), (edge, edges), (sea, flags), (layer, layers), (spin, spins)], more)
    copies = {}
    for n in range(N, -1, -1):
        source = cot if n == N else states.at[n]
        copies[n] = start(
            [(source.at[:, :8, :], own.at[n, 0]), (source.at[:, ROWS - 8 :, :], own.at[n, 1])], sems.at[n]
        )
    back = []
    for e, row in enumerate((0, ROWS - 8)):
        back.append((out_in.at[:, row : row + 8, :], tiles.at[e, :CH]))
        back.append((forcing_in.at[row : row + 8, :], tiles.at[e, CH]))
    back = start(back, more.at[6:])
    wait(first)

    def put(target, at, q, e, s):
        g, k = divmod(q, 16)
        d = depth(q)
        tile = slice(0, 8) if e == 0 else slice(ROWS - 8, ROWS)
        message = (wests, easts)[e]
        here = 4 if e == 0 else 0
        halo = 4 - d if e == 0 else 8
        for j in range(W - 1):
            if q == SEA:
                value = flags[tile, lanes(j)].astype(f32)
            else:
                value = own[q // CH, e, q % CH, :, lanes(j)]
            target[at, j, pl.ds(8 * here + s, 8, stride=8), :] = value
            if d:
                value = message[OFFSET[q] : OFFSET[q] + d, lanes(j)]
                target[at, j, pl.ds(8 * halo + s, d, stride=8), :] = value
        shift = (124 - 8 * k) % 128
        target[at, W - 1, pl.ds(8 * here + s, 8, stride=8), :] = pltpu.roll(edges[g, tile, :], shift, 1)
        corner = pltpu.roll(message[HALO:, lanes(g)], shift, 1)
        target[at, W - 1, pl.ds(8 * (0 if e == 0 else 8) + s, 4, stride=8), :] = corner

    for e in range(2):
        for k in range(L):
            put(mask, 0, SEA, e, 2 * k + e)
            for j in range(W - 1):
                tile = slice(0, 4) if e == 0 else slice(ROWS - 4, ROWS)
                picked[j, pl.ds(2 * k + e, 4, stride=8), :] = layers[tile, lanes(j)]
    wait(copies[N])
    for e in range(2):
        for c in range(CH):
            put(cur, c // L, COT + c, e, 2 * (c % L) + e)

    half = 0.5 * TIME_STEP
    level = lax.broadcasted_iota(jnp.int32, (8, CC), 0) // 2
    sums = []
    for k in range(L):
        sums.append(gravities[k] if k == 0 else sums[-1] + gravities[k])
    couple = []
    for m in range(L):
        weight = jnp.zeros((8, CC), f32)
        for k in range(L):
            weight = jnp.where(level == k, half * sums[min(k, (k - m) % L)], weight)
        couple.append(weight)
    keep = jnp.where(level == L - 1, 1.0 - TIME_STEP * (4.0 * VISCOSITY + BOTTOM_DRAG), 1.0 - TIME_STEP * 4.0 * VISCOSITY)
    edge_lane = lax.broadcasted_iota(jnp.int32, (8, 128), 1)
    inside = jnp.where(edge_lane < 64, place[1], place[2]) > 0

    def row(ref, at, r):
        return jnp.concatenate([ref[at, j, pl.ds(pl.multiple_of(8 * r, 8), 8), :] for j in range(W)], axis=1)

    def set_row(ref, at, r, value):
        for j in range(W):
            ref[at, j, pl.ds(pl.multiple_of(8 * r, 8), 8), :] = value[:, lanes(j)]

    def north(x):
        return pltpu.roll(x, CC - 1, 1)

    def south(x):
        return pltpu.roll(x, 1, 1)

    for r in range(12):
        sea_r = row(mask, 0, r)
        for at in (1, 2):
            set_row(cur, at, r, row(cur, at, r) * sea_r)
    for r in range(4):
        acc[r] = jnp.zeros((8, COLS), f32)

    for i in range(N):
        n = N - 1 - i
        src, dst = (cur, nxt) if i % 2 == 0 else (nxt, cur)
        wait(copies[n])
        for e in range(2):
            for c in range(CH):
                put(fields, c // L, n * CH + c, e, 2 * (c % L) + e)

        for r in range(4):
            idx = jnp.concatenate([picked[j, 8 * r : 8 * r + 8, :] for j in range(W - 1)], axis=1)
            acc[r] = acc[r] + jnp.where(idx == level[:, :COLS], TIME_STEP * row(src, 0, 4 + r)[:, :COLS], 0.0)

        def one_row(r):
            c, p, q = row(src, 0, r), row(src, 1, r), row(src, 2, r)
            h, u, v = row(fields, 0, r), row(fields, 1, r), row(fields, 2, r)
            ce, cw, cn, cs = row(src, 0, r + 1), row(src, 0, r - 1), north(c), south(c)
            pe, pw, pn, ps = row(src, 1, r + 1), row(src, 1, r - 1), north(p), south(p)
            qe, qw, qn, qs = row(src, 2, r + 1), row(src, 2, r - 1), north(q), south(q)
            ue, uw, un, us = row(fields, 1, r + 1), row(fields, 1, r - 1), north(u), south(u)
            ve, vw, vn, vs = row(fields, 2, r + 1), row(fields, 2, r - 1), north(v), south(v)
            dcx = ce - cw
            dcy = cn - cs
            mixed = (pe - pw) + (qn - qs)
            new = (1.0 - 4.0 * TIME_STEP * DIFFUSION) * c + half * (
                u * dcx + v * dcy + (2.0 * DIFFUSION) * ((ce + cw) + (cn + cs))
            )
            for m in range(L):
                new = new + couple[m] * (mixed if m == 0 else pltpu.roll(mixed, 2 * m, 0))
            new = jnp.concatenate([new[:, :COLS], jnp.where(inside, new[:, COLS:], 0.0)], axis=1)
            set_row(dst, 0, r, new)
            a_e = ue + 2.0 * VISCOSITY
            a_w = 2.0 * VISCOSITY - uw
            a_n = vn + 2.0 * VISCOSITY
            a_s = 2.0 * VISCOSITY - vs
            turn = spins[...]
            new_p = keep * p + half * (
                h * dcx
                - turn * q
                - p * (ue - uw)
                - q * (ve - vw)
                + (a_e * pe + a_w * pw)
                + (a_n * pn + a_s * ps)
            )
            new_q = keep * q + half * (
                h * dcy
                + turn * p
                - p * (un - us)
                - q * (vn - vs)
                + (a_e * qe + a_w * qw)
                + (a_n * qn + a_s * qs)
            )
            if n:
                sea_r = row(mask, 0, r)
                new_p, new_q = new_p * sea_r, new_q * sea_r
            set_row(dst, 1, r, new_p)
            set_row(dst, 2, r, new_q)

        def rows_body(b, carry):
            one_row(1 + i + 2 * b)
            one_row(2 + i + 2 * b)
            return carry

        lax.fori_loop(0, 5 - i, rows_body, 0)

    wait(back)
    pairs = []
    for e, start_row in enumerate((0, ROWS - 8)):
        part = slice(0, 4) if e == 0 else slice(4, 8)
        for c in range(CH):
            for j in range(W - 1):
                tiles[e, c, part, lanes(j)] = cur[c // L, j, pl.ds(32 + 2 * (c % L) + e, 4, stride=8), :]
        pairs.append((tiles.at[e, :CH], out.at[:, start_row : start_row + 8, :]))
    copies = start(pairs, more)
    pairs = []
    for e, start_row in enumerate((0, ROWS - 8)):
        for r in range(4):
            total = acc[r]
            total = total + pltpu.roll(total, 4, 0)
            total = total + pltpu.roll(total, 2, 0)
            at = r if e == 0 else 4 + r
            tiles[e, CH, at : at + 1, :] = total[e : e + 1, :]
        pairs.append((tiles.at[e, CH], forcing.at[start_row : start_row + 8, :]))
    copies = copies + start(pairs, more.at[2:])
    wait(copies)


VMEM = pl.BlockSpec(memory_space=pltpu.VMEM)
SMEM = pl.BlockSpec(memory_space=pltpu.SMEM)
ANY = pl.BlockSpec(memory_space=pl.ANY)
HBM = pl.BlockSpec(memory_space=pltpu.HBM)
DMA = pltpu.SemaphoreType.DMA
shape = jax.ShapeDtypeStruct


def ring_scratch(rows):
    T = rows // 8
    return [
        pltpu.VMEM((PLANES, W, rows, 128), f32),
        pltpu.VMEM((CH, T, 8, CC), f32),
        pltpu.VMEM((CH, T, 8, CC), f32),
        pltpu.VMEM((L, T, 8, CC), f32),
        pltpu.VMEM((T, 8, CC), f32),
        pltpu.VMEM((W, rows, 128), jnp.int32),
        pltpu.VMEM((ROWS, COLS), jnp.int32),
        pltpu.VMEM((8, CC), f32),
        pltpu.VMEM((GROUPS, ROWS, 128), f32),
    ]


def per_device(saved_states, final_cotangent, gravities, sea_mask, layer_index):
    lons, lats = lax.axis_size("lon"), lax.axis_size("lat")
    lat = lax.axis_index("lat")
    lane = jnp.arange(CC, dtype=jnp.int32)
    lane = jnp.where(lane < COLS + 64, lane, lane - CC)
    lat_rows = (lat * COLS + lane).astype(f32)
    spin = 2.0 * jnp.sin(jnp.pi * ((lat_rows + 0.5) / (lats * COLS) - 0.5))
    spin = jnp.broadcast_to(spin[None], (8, CC))
    place = jnp.stack([lat % 2, (lat < lats - 1).astype(jnp.int32), (lat > 0).astype(jnp.int32)])

    strips = pl.pallas_call(
        strip_pack_kernel,
        out_shape=shape((GROUPS, ROWS, 128), f32),
        in_specs=[HBM] * 3,
        out_specs=VMEM,
        scratch_shapes=[
            pltpu.VMEM((N + 1, CH, ROWS, 128), f32),
            pltpu.VMEM((N + 1, CH, ROWS, 128), f32),
            pltpu.VMEM((ROWS, COLS), jnp.int32),
            DMA((5,)),
        ],
        compiler_params=pltpu.CompilerParams(vmem_limit_bytes=60 << 20),
    )(saved_states, final_cotangent, sea_mask)

    def at(i, j):
        return (i % lons) * lats + j

    def swap(x, first):
        pairs = [(at(i, j), at(i, j + 1)) for i in range(lons) for j in range(first, lats - 1, 2)]
        return lax.ppermute(x, ("lon", "lat"), pairs + [(b, a) for a, b in pairs])

    def shift(x, by):
        return lax.ppermute(x, "lon", [(i, (i + by) % lons) for i in range(lons)])

    pair, middle = swap(strips, 0), swap(strips, 1)
    east, west, edge = pl.pallas_call(
        row_pack_kernel,
        out_shape=[shape((MESSAGE, COLS), f32), shape((MESSAGE, COLS), f32), shape((GROUPS, ROWS, 128), f32)],
        in_specs=[SMEM, HBM, HBM, HBM, VMEM, VMEM],
        out_specs=[VMEM] * 3,
        scratch_shapes=[
            pltpu.VMEM((N + 1, CH, 8, COLS), f32),
            pltpu.VMEM((N + 1, CH, 8, COLS), f32),
            pltpu.VMEM((ROWS, COLS), jnp.int32),
            DMA((5,)),
        ],
        compiler_params=pltpu.CompilerParams(vmem_limit_bytes=53 << 20),
    )(place, saved_states, final_cotangent, sea_mask, pair, middle)
    from_west, from_east = shift(east, 1), shift(west, -1)

    outs = [shape((CH, ROWS, COLS), f32), shape((ROWS, COLS), f32)]
    out, forcing = pl.pallas_call(
        main_kernel,
        out_shape=outs,
        in_specs=[SMEM, SMEM] + [HBM] * 4 + [ANY] * 2,
        out_specs=[HBM, HBM],
        scratch_shapes=ring_scratch(ROWS) + [DMA((N + 1, W - 1, 1)), DMA((16,))],
        compiler_params=pltpu.CompilerParams(vmem_limit_bytes=53 << 20),
        cost_estimate=pl.CostEstimate(flops=160_000_000, bytes_accessed=24_000_000, transcendentals=0),
    )(place, gravities, saved_states, final_cotangent, sea_mask, layer_index, spin, edge)

    return pl.pallas_call(
        rim_kernel,
        out_shape=outs,
        in_specs=[SMEM, SMEM] + [HBM] * 4 + [ANY] * 4 + [HBM] * 2,
        out_specs=[HBM, HBM],
        scratch_shapes=[
            pltpu.VMEM((N + 1, 2, CH, 8, COLS), f32),
            pltpu.VMEM((3, W, 96, 128), f32),
            pltpu.VMEM((3, W, 96, 128), f32),
            pltpu.VMEM((3, W, 96, 128), f32),
            pltpu.VMEM((1, W, 96, 128), f32),
            pltpu.VMEM((4, 8, COLS), f32),
            pltpu.VMEM((W - 1, 32, 128), jnp.int32),
            pltpu.VMEM((ROWS, COLS), jnp.int32),
            pltpu.VMEM((ROWS, COLS), jnp.int32),
            pltpu.VMEM((8, CC), f32),
            pltpu.VMEM((GROUPS, ROWS, 128), f32),
            pltpu.VMEM((MESSAGE, COLS), f32),
            pltpu.VMEM((MESSAGE, COLS), f32),
            pltpu.VMEM((2, CH + 1, 8, COLS), f32),
            DMA((N + 1, 2)),
            DMA((10,)),
        ],
        input_output_aliases={10: 0, 11: 1},
        compiler_params=pltpu.CompilerParams(vmem_limit_bytes=53 << 20),
    )(
        place,
        gravities,
        saved_states,
        final_cotangent,
        sea_mask,
        layer_index,
        spin,
        from_west,
        from_east,
        edge,
        out,
        forcing,
    )


def solution(mesh):
    return jax.shard_map(
        per_device,
        mesh=mesh,
        in_specs=(
            P(None, None, "lon", "lat"),
            P(None, "lon", "lat"),
            P(),
            P("lon", "lat"),
            P("lon", "lat"),
        ),
        out_specs=(P(None, "lon", "lat"), P("lon", "lat")),
        check_vma=False,
    )
```

```python
import jax
import jax.numpy as jnp
from jax import lax
from jax.experimental import pallas as pl
from jax.experimental.pallas import tpu as pltpu
from jax.sharding import PartitionSpec as P

TIME_STEP = 0.3
VISCOSITY = 0.1
DIFFUSION = 0.05
BOTTOM_DRAG = 0.2

L = 4
N = 4
CH = 3 * L
ROWS = 32
COLS = 512
CC = COLS + 128
W = CC // 128

COT = N * CH
SEA = COT + CH
PLANES = SEA + 1
GROUPS = -(-PLANES // 16)
f32 = jnp.float32


def place_of():
    lon, lat = lax.axis_index("lon"), lax.axis_index("lat")
    return lat % 2, lat < lax.axis_size("lat") - 1, lat > 0, lon == 0


def lanes(j):
    return slice(128 * j, 128 * j + 128)


def depth(q):
    if q >= COT:
        return N
    n, c = divmod(q, CH)
    return n + 1 if c >= L else n


OFFSET = {}
HALO = 0
for _q in sorted(range(SEA), key=lambda q: -depth(q)) + [SEA]:
    if depth(_q):
        OFFSET[_q] = HALO
        HALO += depth(_q)
MESSAGE = HALO + N
TAIL = MESSAGE - 8
assert OFFSET[SEA] == TAIL


def start(pairs, sems):
    copies = [pltpu.make_async_copy(a, b, sems.at[i]) for i, (a, b) in enumerate(pairs)]
    for copy in copies:
        copy.start()
    return copies


def wait(copies):
    for copy in copies:
        copy.wait()


def strip_pack_kernel(states, cot, sea, strips, left, right, flags, sems):
    pairs = [(sea, flags)]
    for buf, cols in ((left, slice(0, 128)), (right, slice(COLS - 128, COLS))):
        pairs.append((states.at[:, :, :, cols], buf.at[:N]))
        pairs.append((cot.at[:, :, cols], buf.at[N]))
    wait(start(pairs, sems))
    lane = lax.broadcasted_iota(jnp.int32, (ROWS, 128), 1)
    for g in range(GROUPS):
        total = jnp.zeros((ROWS, 128), f32)
        for k in range(16):
            q = g * 16 + k
            if q >= PLANES:
                continue
            if q == SEA:
                first, last = flags[:, lanes(0)].astype(f32), flags[:, lanes(W - 2)].astype(f32)
            else:
                first, last = left[q // CH, q % CH], right[q // CH, q % CH]
            both = pltpu.roll(jnp.where(lane >= 124, last, first), (8 * k + 4) % 128, 1)
            total = jnp.where(lane // 8 == k, both, total)
        strips[g] = total


def row_pack_kernel(states, cot, east, west, top, bottom, sems):
    pairs = []
    for buf, rows in ((bottom, slice(ROWS - 8, ROWS)), (top, slice(0, 8))):
        pairs.append((states.at[:, :, rows, :], buf.at[:N]))
        pairs.append((cot.at[:, rows, :], buf.at[N]))
    wait(start(pairs, sems))
    for q, row in OFFSET.items():
        if q == SEA:
            continue
        d = depth(q)
        east[row : row + d] = bottom[q // CH, q % CH, 8 - d :]
        west[row : row + d] = top[q // CH, q % CH, :d]


def attach_kernel(sea, pair, middle, east_in, west_in, edge, east, west, flags, tails, sems):
    copies = start([(sea, flags)], sems)
    odd = place_of()[0] == 1
    south = lax.broadcasted_iota(jnp.int32, (ROWS, 128), 1) % 8 < 4
    for g in range(GROUPS):
        merged = jnp.where(south == odd, pair[g], middle[g])
        edge[g] = merged
        tails[0, N:, lanes(g)] = merged[ROWS - N :]
        tails[1, N:, lanes(g)] = merged[:N]
    wait(copies)
    tails[0, :N, :] = flags[ROWS - N :].astype(f32)
    tails[1, :N, :] = flags[:N].astype(f32)
    wait(start([(tails.at[0], east.at[TAIL:, :]), (tails.at[1], west.at[TAIL:, :])], sems))


def fill_columns(planes, edge, blocks):
    for source, target, count in blocks:
        for q in range(PLANES):
            g, k = divmod(q, 16)
            planes[q, W - 1, target : target + count, :] = pltpu.roll(
                edge[g, source : source + count, :], (124 - 8 * k) % 128, 1
            )


def own_copies(n, source, planes, blocks, sems):
    return [
        pltpu.make_async_copy(
            source.at[:, row : row + count, lanes(j)],
            planes.at[pl.ds(n * CH, CH), j, target : target + count, :],
            sems.at[n, j, i],
        )
        for i, (row, target, count) in enumerate(blocks)
        for j in range(W - 1)
    ]


def adjoint_steps(rows, arrive, gravities, spin, planes, picked, cur, nxt, mixed, acc):
    T = rows // 8
    half = 0.5 * TIME_STEP

    def ring(t):
        return pl.ds(t, 8, stride=T)

    def read(q, t):
        return jnp.concatenate([planes[q, j, ring(t), :] for j in range(W)], axis=1)

    def write(q, t, value):
        for j in range(W - 1):
            planes[q, j, ring(t), :] = value[:, lanes(j)]

    for t in range(T):
        sea_t = read(SEA, t)
        for c in range(CH):
            value = read(COT + c, t)
            cur[c, t] = value if c < L else value * sea_t
        acc[t] = jnp.zeros((8, CC), f32)

    place = place_of()
    edge_lane = lax.broadcasted_iota(jnp.int32, (8, 128), 1)
    inside = (edge_lane < 64) & place[1] | (edge_lane >= 64) & place[2]

    def north(x):
        return pltpu.roll(x, CC - 1, 1)

    def south(x):
        return pltpu.roll(x, 1, 1)

    def east(load, t):
        return load(t + 1) if t + 1 < T else pltpu.roll(load(0), 7, 0)

    def west(load, t):
        return load(t - 1) if t > 0 else pltpu.roll(load(T - 1), 1, 0)

    def one_step(index, src, dst):
        n = N - 1 - index
        arrive(n)

        def layer_body(k, carry):
            load_h = lambda t: read(n * CH + k, t)
            load_u = lambda t: read(n * CH + L + k, t)
            load_v = lambda t: read(n * CH + 2 * L + k, t)
            load_c = lambda t: src[k, t]
            load_p = lambda t: src[L + k, t]
            load_q = lambda t: src[2 * L + k, t]
            drag = jnp.where(k == L - 1, BOTTOM_DRAG, 0.0)
            keep = 1.0 - TIME_STEP * (4.0 * VISCOSITY + drag)
            turn = spin[...]
            for t in range(T):
                c, p, q = load_c(t), load_p(t), load_q(t)
                h, u, v = load_h(t), load_u(t), load_v(t)
                ce, cw, cn, cs = east(load_c, t), west(load_c, t), north(c), south(c)
                dcx = ce - cw
                dcy = cn - cs
                pe, pw, pn, ps = east(load_p, t), west(load_p, t), north(p), south(p)
                qe, qw, qn, qs = east(load_q, t), west(load_q, t), north(q), south(q)
                mixed[k, t] = (pe - pw) + (qn - qs)
                dst[k, t] = (1.0 - 4.0 * TIME_STEP * DIFFUSION) * c + half * (
                    u * dcx + v * dcy + (2.0 * DIFFUSION) * ((ce + cw) + (cn + cs))
                )
                ue, uw, un, us = east(load_u, t), west(load_u, t), north(u), south(u)
                ve, vw, vn, vs = east(load_v, t), west(load_v, t), north(v), south(v)
                a_e = ue + 2.0 * VISCOSITY
                a_w = 2.0 * VISCOSITY - uw
                a_n = vn + 2.0 * VISCOSITY
                a_s = 2.0 * VISCOSITY - vs
                new_p = keep * p + half * (
                    h * dcx
                    - turn * q
                    - p * (ue - uw)
                    - q * (ve - vw)
                    + (a_e * pe + a_w * pw)
                    + (a_n * pn + a_s * ps)
                )
                new_q = keep * q + half * (
                    h * dcy
                    + turn * p
                    - p * (un - us)
                    - q * (vn - vs)
                    + (a_e * qe + a_w * qw)
                    + (a_n * qn + a_s * qs)
                )
                mask = jnp.where(n == 0, 1.0, read(SEA, t))
                dst[L + k, t] = new_p * mask
                dst[2 * L + k, t] = new_q * mask
            return carry

        lax.fori_loop(0, L, layer_body, 0)
        for t in range(T):
            idx = jnp.concatenate([picked[j, ring(t), :] for j in range(W)], axis=1)
            chosen = jnp.zeros((8, CC), f32)
            for k in range(L):
                chosen = jnp.where(idx == k, src[k, t], chosen)
            acc[t] = acc[t] + TIME_STEP * chosen
            total = mixed[L - 1, t]
            tails = [total]
            for k in range(L - 2, -1, -1):
                total = total + mixed[k, t]
                tails.insert(0, total)
            head = None
            for k in range(L):
                term = (half * gravities[k]) * tails[k]
                head = term if head is None else head + term
                new = dst[k, t] + head
                dst[k, t, :, :COLS] = new[:, :COLS]
                dst[k, t, :, COLS:] = jnp.where(inside, new[:, COLS:], 0.0)

    def two_steps(i, carry):
        one_step(2 * i, cur, nxt)
        one_step(2 * i + 1, nxt, cur)
        return carry

    lax.fori_loop(0, N // 2, two_steps, 0)

    for t in range(T):
        for c in range(CH):
            write(COT + c, t, cur[c, t])
        write(SEA, t, acc[t])


def layer_copies(layer, picked, blocks):
    return [
        (layer.at[row : row + count, lanes(j)], picked.at[j, target : target + count, :])
        for row, target, count in blocks
        for j in range(W - 1)
    ]


def main_kernel(
    early,
    gravities_in,
    states,
    cot,
    sea,
    layer,
    spin,
    edge,
    out,
    forcing,
    planes,
    cur,
    nxt,
    mixed,
    acc,
    picked,
    flags,
    spins,
    edges,
    gravities,
    sems,
    more,
):
    @pl.when(place_of()[3] == early)
    def _():
        blocks = [(0, 0, ROWS)]
        first = start([(gravities_in, gravities), (sea, flags), (edge, edges), (spin, spins)] + layer_copies(layer, picked, blocks), more)
        copies = [own_copies(N, cot, planes, blocks, sems)]
        for n in range(N - 1, -1, -1):
            copies.append(own_copies(n, states.at[n], planes, blocks, sems))
        for group in copies:
            for copy in group:
                copy.start()
        wait(first)
        for j in range(W - 1):
            planes[SEA, j, :ROWS, :] = flags[:, lanes(j)].astype(f32)
        fill_columns(planes, edges, blocks)
        wait(copies[0])
        adjoint_steps(
            ROWS,
            lambda n: wait(own_copies(n, states.at[n], planes, blocks, sems)),
            gravities,
            spins,
            planes,
            picked,
            cur,
            nxt,
            mixed,
            acc,
        )
        pairs = []
        for j in range(W - 1):
            pairs.append((planes.at[COT : COT + CH, j, :ROWS, :], out.at[:, :, lanes(j)]))
            pairs.append((planes.at[SEA, j, :ROWS, :], forcing.at[:, lanes(j)]))
        wait(start(pairs, more))


def early_kernel(gravities, states, cot, sea, layer, spin, edge, west_in, out, forcing, west, *scratch):
    main_kernel(True, gravities, states, cot, sea, layer, spin, edge, out, forcing, *scratch)


def late_kernel(gravities, states, cot, sea, layer, spin, edge, out_in, forcing_in, out, forcing, *scratch):
    main_kernel(False, gravities, states, cot, sea, layer, spin, edge, out, forcing, *scratch)


def rim_kernel(
    gravities_in,
    states,
    cot,
    sea,
    layer,
    spin,
    from_west,
    from_east,
    edge,
    out_in,
    forcing_in,
    out,
    forcing,
    own,
    fields,
    cur,
    nxt,
    mask,
    acc,
    picked,
    flags,
    layers,
    spins,
    edges,
    wests,
    easts,
    tiles,
    gravities,
    sems,
    more,
):
    first = start([(from_west, wests), (from_east, easts), (edge, edges), (sea, flags), (layer, layers), (spin, spins), (gravities_in, gravities)], more)
    copies = {}

    def fetch(n):
        source = cot if n == N else states.at[n]
        copies[n] = start(
            [(source.at[:, :8, :], own.at[n, 0]), (source.at[:, ROWS - 8 :, :], own.at[n, 1])], sems.at[n]
        )

    fetch(N)
    fetch(N - 1)
    wait(first)
    for n in range(N - 2, -1, -1):
        fetch(n)
    back = []
    for e, row in enumerate((0, ROWS - 8)):
        back.append((out_in.at[:, row : row + 8, :], tiles.at[e, :CH]))
        back.append((forcing_in.at[row : row + 8, :], tiles.at[e, CH]))
    back = start(back, more.at[7:])

    def put(target, at, q, e, s):
        g, k = divmod(q, 16)
        d = depth(q)
        tile = slice(0, 8) if e == 0 else slice(ROWS - 8, ROWS)
        message = (wests, easts)[e]
        here = 4 if e == 0 else 0
        halo = 4 - d if e == 0 else 8
        for j in range(W - 1):
            if q == SEA:
                value = flags[tile, lanes(j)].astype(f32)
            else:
                value = own[q // CH, e, q % CH, :, lanes(j)]
            target[at, j, pl.ds(8 * here + s, 8, stride=8), :] = value
            if d:
                value = message[OFFSET[q] : OFFSET[q] + d, lanes(j)]
                target[at, j, pl.ds(8 * halo + s, d, stride=8), :] = value
        shift = (124 - 8 * k) % 128
        target[at, W - 1, pl.ds(8 * here + s, 8, stride=8), :] = pltpu.roll(edges[g, tile, :], shift, 1)
        corner = pltpu.roll(message[HALO:, lanes(g)], shift, 1)
        target[at, W - 1, pl.ds(8 * (0 if e == 0 else 8) + s, 4, stride=8), :] = corner

    for e in range(2):
        for k in range(L):
            put(mask, 0, SEA, e, 2 * k + e)
            for j in range(W - 1):
                tile = slice(0, 4) if e == 0 else slice(ROWS - 4, ROWS)
                picked[j, pl.ds(2 * k + e, 4, stride=8), :] = layers[tile, lanes(j)]
    wait(copies[N])
    for e in range(2):
        for c in range(CH):
            put(cur, c // L, COT + c, e, 2 * (c % L) + e)

    half = 0.5 * TIME_STEP
    level = lax.broadcasted_iota(jnp.int32, (8, CC), 0) // 2
    sums = []
    for k in range(L):
        sums.append(gravities[k] if k == 0 else sums[-1] + gravities[k])
    couple = []
    for m in range(L):
        weight = jnp.zeros((8, CC), f32)
        for k in range(L):
            weight = jnp.where(level == k, half * sums[min(k, (k - m) % L)], weight)
        couple.append(weight)
    keep = jnp.where(level == L - 1, 1.0 - TIME_STEP * (4.0 * VISCOSITY + BOTTOM_DRAG), 1.0 - TIME_STEP * 4.0 * VISCOSITY)
    place = place_of()
    edge_lane = lax.broadcasted_iota(jnp.int32, (8, 128), 1)
    inside = (edge_lane < 64) & place[1] | (edge_lane >= 64) & place[2]

    def row(ref, at, r):
        return jnp.concatenate([ref[at, j, pl.ds(pl.multiple_of(8 * r, 8), 8), :] for j in range(W)], axis=1)

    def set_row(ref, at, r, value):
        for j in range(W):
            ref[at, j, pl.ds(pl.multiple_of(8 * r, 8), 8), :] = value[:, lanes(j)]

    def north(x):
        return pltpu.roll(x, CC - 1, 1)

    def south(x):
        return pltpu.roll(x, 1, 1)

    for r in range(12):
        sea_r = row(mask, 0, r)
        for at in (1, 2):
            set_row(cur, at, r, row(cur, at, r) * sea_r)
    for r in range(4):
        acc[r] = jnp.zeros((8, COLS), f32)

    for i in range(N):
        n = N - 1 - i
        src, dst = (cur, nxt) if i % 2 == 0 else (nxt, cur)
        wait(copies[n])
        for e in range(2):
            for c in range(CH):
                put(fields, c // L, n * CH + c, e, 2 * (c % L) + e)

        for r in range(4):
            idx = jnp.concatenate([picked[j, 8 * r : 8 * r + 8, :] for j in range(W - 1)], axis=1)
            acc[r] = acc[r] + jnp.where(idx == level[:, :COLS], TIME_STEP * row(src, 0, 4 + r)[:, :COLS], 0.0)

        def one_row(r):
            c, p, q = row(src, 0, r), row(src, 1, r), row(src, 2, r)
            h, u, v = row(fields, 0, r), row(fields, 1, r), row(fields, 2, r)
            ce, cw, cn, cs = row(src, 0, r + 1), row(src, 0, r - 1), north(c), south(c)
            pe, pw, pn, ps = row(src, 1, r + 1), row(src, 1, r - 1), north(p), south(p)
            qe, qw, qn, qs = row(src, 2, r + 1), row(src, 2, r - 1), north(q), south(q)
            ue, uw, un, us = row(fields, 1, r + 1), row(fields, 1, r - 1), north(u), south(u)
            ve, vw, vn, vs = row(fields, 2, r + 1), row(fields, 2, r - 1), north(v), south(v)
            dcx = ce - cw
            dcy = cn - cs
            mixed = (pe - pw) + (qn - qs)
            new = (1.0 - 4.0 * TIME_STEP * DIFFUSION) * c + half * (
                u * dcx + v * dcy + (2.0 * DIFFUSION) * ((ce + cw) + (cn + cs))
            )
            for m in range(L):
                new = new + couple[m] * (mixed if m == 0 else pltpu.roll(mixed, 2 * m, 0))
            new = jnp.concatenate([new[:, :COLS], jnp.where(inside, new[:, COLS:], 0.0)], axis=1)
            set_row(dst, 0, r, new)
            a_e = ue + 2.0 * VISCOSITY
            a_w = 2.0 * VISCOSITY - uw
            a_n = vn + 2.0 * VISCOSITY
            a_s = 2.0 * VISCOSITY - vs
            turn = spins[...]
            new_p = keep * p + half * (
                h * dcx
                - turn * q
                - p * (ue - uw)
                - q * (ve - vw)
                + (a_e * pe + a_w * pw)
                + (a_n * pn + a_s * ps)
            )
            new_q = keep * q + half * (
                h * dcy
                + turn * p
                - p * (un - us)
                - q * (vn - vs)
                + (a_e * qe + a_w * qw)
                + (a_n * qn + a_s * qs)
            )
            if n:
                sea_r = row(mask, 0, r)
                new_p, new_q = new_p * sea_r, new_q * sea_r
            set_row(dst, 1, r, new_p)
            set_row(dst, 2, r, new_q)

        def rows_body(b, carry):
            one_row(1 + i + 2 * b)
            one_row(2 + i + 2 * b)
            return carry

        lax.fori_loop(0, 5 - i, rows_body, 0)

    wait(back)
    pairs = []
    for e, start_row in enumerate((0, ROWS - 8)):
        part = slice(0, 4) if e == 0 else slice(4, 8)
        for c in range(CH):
            for j in range(W - 1):
                tiles[e, c, part, lanes(j)] = cur[c // L, j, pl.ds(32 + 2 * (c % L) + e, 4, stride=8), :]
        pairs.append((tiles.at[e, :CH], out.at[:, start_row : start_row + 8, :]))
    copies = start(pairs, more)
    pairs = []
    for e, start_row in enumerate((0, ROWS - 8)):
        for r in range(4):
            total = acc[r]
            total = total + pltpu.roll(total, 4, 0)
            total = total + pltpu.roll(total, 2, 0)
            at = r if e == 0 else 4 + r
            tiles[e, CH, at : at + 1, :] = total[e : e + 1, :]
        pairs.append((tiles.at[e, CH], forcing.at[start_row : start_row + 8, :]))
    copies = copies + start(pairs, more.at[2:])
    wait(copies)


VMEM = pl.BlockSpec(memory_space=pltpu.VMEM)
ANY = pl.BlockSpec(memory_space=pl.ANY)
HBM = pl.BlockSpec(memory_space=pltpu.HBM)
DMA = pltpu.SemaphoreType.DMA
shape = jax.ShapeDtypeStruct


def ring_scratch(rows):
    T = rows // 8
    return [
        pltpu.VMEM((PLANES, W, rows, 128), f32),
        pltpu.VMEM((CH, T, 8, CC), f32),
        pltpu.VMEM((CH, T, 8, CC), f32),
        pltpu.VMEM((L, T, 8, CC), f32),
        pltpu.VMEM((T, 8, CC), f32),
        pltpu.VMEM((W, rows, 128), jnp.int32),
        pltpu.VMEM((ROWS, COLS), jnp.int32),
        pltpu.VMEM((8, CC), f32),
        pltpu.VMEM((GROUPS, ROWS, 128), f32),
    ]


def per_device(saved_states, final_cotangent, gravities, sea_mask, layer_index):
    lons, lats = lax.axis_size("lon"), lax.axis_size("lat")
    lat = lax.axis_index("lat")
    lane = jnp.arange(CC, dtype=jnp.int32)
    lane = jnp.where(lane < COLS + 64, lane, lane - CC)
    lat_rows = (lat * COLS + lane).astype(f32)
    spin = 2.0 * jnp.sin(jnp.pi * ((lat_rows + 0.5) / (lats * COLS) - 0.5))
    spin = jnp.broadcast_to(spin[None], (8, CC))
    strips = pl.pallas_call(
        strip_pack_kernel,
        out_shape=shape((GROUPS, ROWS, 128), f32),
        in_specs=[HBM] * 3,
        out_specs=VMEM,
        scratch_shapes=[
            pltpu.VMEM((N + 1, CH, ROWS, 128), f32),
            pltpu.VMEM((N + 1, CH, ROWS, 128), f32),
            pltpu.VMEM((ROWS, COLS), jnp.int32),
            DMA((5,)),
        ],
        compiler_params=pltpu.CompilerParams(vmem_limit_bytes=60 << 20),
    )(saved_states, final_cotangent, sea_mask)

    def at(i, j):
        return (i % lons) * lats + j

    def swap(x, first):
        pairs = [(at(i, j), at(i, j + 1)) for i in range(lons) for j in range(first, lats - 1, 2)]
        return lax.ppermute(x, ("lon", "lat"), pairs + [(b, a) for a, b in pairs])

    def shift(x, by):
        return lax.ppermute(x, "lon", [(i, (i + by) % lons) for i in range(lons)])

    pair, middle = swap(strips, 0), swap(strips, 1)
    east, west = pl.pallas_call(
        row_pack_kernel,
        out_shape=[shape((MESSAGE, COLS), f32)] * 2,
        in_specs=[HBM] * 2,
        out_specs=[VMEM] * 2,
        scratch_shapes=[
            pltpu.VMEM((N + 1, CH, 8, COLS), f32),
            pltpu.VMEM((N + 1, CH, 8, COLS), f32),
            DMA((4,)),
        ],
        compiler_params=pltpu.CompilerParams(vmem_limit_bytes=53 << 20),
    )(saved_states, final_cotangent)
    edge, east, west = pl.pallas_call(
        attach_kernel,
        out_shape=[shape((GROUPS, ROWS, 128), f32)] + [shape((MESSAGE, COLS), f32)] * 2,
        in_specs=[HBM, VMEM, VMEM, HBM, HBM],
        out_specs=[VMEM, HBM, HBM],
        scratch_shapes=[pltpu.VMEM((ROWS, COLS), jnp.int32), pltpu.VMEM((2, 8, COLS), f32), DMA((2,))],
        input_output_aliases={3: 1, 4: 2},
        compiler_params=pltpu.CompilerParams(vmem_limit_bytes=53 << 20),
    )(sea_mask, pair, middle, east, west)

    outs = [shape((CH, ROWS, COLS), f32), shape((ROWS, COLS), f32)]
    main = dict(
        scratch_shapes=ring_scratch(ROWS) + [pltpu.SMEM((L,), f32), DMA((N + 1, W - 1, 1)), DMA((16,))],
        compiler_params=pltpu.CompilerParams(vmem_limit_bytes=53 << 20),
        cost_estimate=pl.CostEstimate(flops=160_000_000, bytes_accessed=24_000_000, transcendentals=0),
    )
    fixed = (gravities, saved_states, final_cotangent, sea_mask, layer_index, spin, edge)
    specs = [ANY] + [HBM] * 4 + [ANY] * 2
    from_west = shift(east, 1)
    out, forcing, west = pl.pallas_call(
        early_kernel,
        out_shape=outs + [shape((MESSAGE, COLS), f32)],
        in_specs=specs + [HBM],
        out_specs=[HBM] * 3,
        input_output_aliases={7: 2},
        **main,
    )(*fixed, west)
    from_east = shift(west, -1)
    out, forcing = pl.pallas_call(
        late_kernel,
        out_shape=outs,
        in_specs=specs + [HBM] * 2,
        out_specs=[HBM] * 2,
        input_output_aliases={7: 0, 8: 1},
        **main,
    )(*fixed, out, forcing)

    return pl.pallas_call(
        rim_kernel,
        out_shape=outs,
        in_specs=[ANY] + [HBM] * 4 + [ANY] * 4 + [HBM] * 2,
        out_specs=[HBM, HBM],
        scratch_shapes=[
            pltpu.VMEM((N + 1, 2, CH, 8, COLS), f32),
            pltpu.VMEM((3, W, 96, 128), f32),
            pltpu.VMEM((3, W, 96, 128), f32),
            pltpu.VMEM((3, W, 96, 128), f32),
            pltpu.VMEM((1, W, 96, 128), f32),
            pltpu.VMEM((4, 8, COLS), f32),
            pltpu.VMEM((W - 1, 32, 128), jnp.int32),
            pltpu.VMEM((ROWS, COLS), jnp.int32),
            pltpu.VMEM((ROWS, COLS), jnp.int32),
            pltpu.VMEM((8, CC), f32),
            pltpu.VMEM((GROUPS, ROWS, 128), f32),
            pltpu.VMEM((MESSAGE, COLS), f32),
            pltpu.VMEM((MESSAGE, COLS), f32),
            pltpu.VMEM((2, CH + 1, 8, COLS), f32),
            pltpu.SMEM((L,), f32),
            DMA((N + 1, 2)),
            DMA((11,)),
        ],
        input_output_aliases={9: 0, 10: 1},
        compiler_params=pltpu.CompilerParams(vmem_limit_bytes=53 << 20),
    )(
        gravities,
        saved_states,
        final_cotangent,
        sea_mask,
        layer_index,
        spin,
        from_west,
        from_east,
        edge,
        out,
        forcing,
    )


def solution(mesh):
    return jax.shard_map(
        per_device,
        mesh=mesh,
        in_specs=(
            P(None, None, "lon", "lat"),
            P(None, "lon", "lat"),
            P(),
            P("lon", "lat"),
            P("lon", "lat"),
        ),
        out_specs=(P(None, "lon", "lat"), P("lon", "lat")),
        check_vma=False,
    )
```

```python
import jax
import jax.numpy as jnp
from jax import lax
from jax.experimental import pallas as pl
from jax.experimental.pallas import tpu as pltpu
from jax.sharding import PartitionSpec as P

TIME_STEP = 0.3
VISCOSITY = 0.1
DIFFUSION = 0.05
BOTTOM_DRAG = 0.2

L = 4
N = 4
CH = 3 * L
ROWS = 32
COLS = 512
CC = COLS + 128
W = CC // 128

COT = N * CH
SEA = COT + CH
PLANES = SEA + 1
GROUPS = -(-PLANES // 16)
f32 = jnp.float32


def place_of():
    lon, lat = lax.axis_index("lon"), lax.axis_index("lat")
    return lat % 2, lat < lax.axis_size("lat") - 1, lat > 0, lon == 0


def lanes(j):
    return slice(128 * j, 128 * j + 128)


def depth(q):
    if q >= COT:
        return N
    n, c = divmod(q, CH)
    return n + 1 if c >= L else n


OFFSET = {}
HALO = 0
for _q in sorted(range(SEA), key=lambda q: -depth(q)) + [SEA]:
    if depth(_q):
        OFFSET[_q] = HALO
        HALO += depth(_q)
MESSAGE = HALO + N
TAIL = MESSAGE - 8
assert OFFSET[SEA] == TAIL


def start(pairs, sems):
    copies = [pltpu.make_async_copy(a, b, sems.at[i]) for i, (a, b) in enumerate(pairs)]
    for copy in copies:
        copy.start()
    return copies


def wait(copies):
    for copy in copies:
        copy.wait()


def strip_pack_kernel(states, cot, sea, strips, left, right, flags, sems):
    pairs = [(sea, flags)]
    for buf, cols in ((left, slice(0, 128)), (right, slice(COLS - 128, COLS))):
        pairs.append((states.at[:, :, :, cols], buf.at[:N]))
        pairs.append((cot.at[:, :, cols], buf.at[N]))
    wait(start(pairs, sems))
    lane = lax.broadcasted_iota(jnp.int32, (ROWS, 128), 1)
    for g in range(GROUPS):
        total = jnp.zeros((ROWS, 128), f32)
        for k in range(16):
            q = g * 16 + k
            if q >= PLANES:
                continue
            if q == SEA:
                first, last = flags[:, lanes(0)].astype(f32), flags[:, lanes(W - 2)].astype(f32)
            else:
                first, last = left[q // CH, q % CH], right[q // CH, q % CH]
            both = pltpu.roll(jnp.where(lane >= 124, last, first), (8 * k + 4) % 128, 1)
            total = jnp.where(lane // 8 == k, both, total)
        strips[g] = total


def row_pack_kernel(states, cot, east, west, own, sems):
    pairs = []
    for e, rows in enumerate((slice(0, 8), slice(ROWS - 8, ROWS))):
        pairs.append((states.at[:, :, rows, :], own.at[e, :N]))
        pairs.append((cot.at[:, rows, :], own.at[e, N]))
    wait(start(pairs, sems))
    for q, row in OFFSET.items():
        if q == SEA:
            continue
        d = depth(q)
        east[row : row + d] = own[1, q // CH, q % CH, 8 - d :]
        west[row : row + d] = own[0, q // CH, q % CH, :d]


def attach_kernel(sea, pair, middle, east_in, west_in, edge, east, west, flags, tails, sems):
    copies = start([(sea, flags)], sems)
    odd = place_of()[0] == 1
    south = lax.broadcasted_iota(jnp.int32, (ROWS, 128), 1) % 8 < 4
    for g in range(GROUPS):
        merged = jnp.where(south == odd, pair[g], middle[g])
        edge[g] = merged
        tails[0, N:, lanes(g)] = merged[ROWS - N :]
        tails[1, N:, lanes(g)] = merged[:N]
    wait(copies)
    tails[0, :N, :] = flags[ROWS - N :].astype(f32)
    tails[1, :N, :] = flags[:N].astype(f32)
    wait(start([(tails.at[0], east.at[TAIL:, :]), (tails.at[1], west.at[TAIL:, :])], sems))


def fill_columns(planes, edge, blocks):
    for source, target, count in blocks:
        for q in range(PLANES):
            g, k = divmod(q, 16)
            planes[q, W - 1, target : target + count, :] = pltpu.roll(
                edge[g, source : source + count, :], (124 - 8 * k) % 128, 1
            )


def own_copies(n, source, planes, blocks, sems):
    return [
        pltpu.make_async_copy(
            source.at[:, row : row + count, lanes(j)],
            planes.at[pl.ds(n * CH, CH), j, target : target + count, :],
            sems.at[n, j, i],
        )
        for i, (row, target, count) in enumerate(blocks)
        for j in range(W - 1)
    ]


def adjoint_steps(rows, arrive, gravities, spin, planes, picked, cur, nxt, mixed, acc):
    T = rows // 8
    half = 0.5 * TIME_STEP

    def ring(t):
        return pl.ds(t, 8, stride=T)

    def read(q, t):
        return jnp.concatenate([planes[q, j, ring(t), :] for j in range(W)], axis=1)

    def write(q, t, value):
        for j in range(W - 1):
            planes[q, j, ring(t), :] = value[:, lanes(j)]

    for t in range(T):
        sea_t = read(SEA, t)
        for c in range(CH):
            value = read(COT + c, t)
            cur[c, t] = value if c < L else value * sea_t
        acc[t] = jnp.zeros((8, CC), f32)

    place = place_of()
    edge_lane = lax.broadcasted_iota(jnp.int32, (8, 128), 1)
    inside = (edge_lane < 64) & place[1] | (edge_lane >= 64) & place[2]

    def north(x):
        return pltpu.roll(x, CC - 1, 1)

    def south(x):
        return pltpu.roll(x, 1, 1)

    def east(load, t):
        return load(t + 1) if t + 1 < T else pltpu.roll(load(0), 7, 0)

    def west(load, t):
        return load(t - 1) if t > 0 else pltpu.roll(load(T - 1), 1, 0)

    def one_step(index, src, dst):
        n = N - 1 - index
        arrive(n)

        def layer_body(k, carry):
            load_h = lambda t: read(n * CH + k, t)
            load_u = lambda t: read(n * CH + L + k, t)
            load_v = lambda t: read(n * CH + 2 * L + k, t)
            load_c = lambda t: src[k, t]
            load_p = lambda t: src[L + k, t]
            load_q = lambda t: src[2 * L + k, t]
            drag = jnp.where(k == L - 1, BOTTOM_DRAG, 0.0)
            keep = 1.0 - TIME_STEP * (4.0 * VISCOSITY + drag)
            turn = spin[...]
            for t in range(T):
                c, p, q = load_c(t), load_p(t), load_q(t)
                h, u, v = load_h(t), load_u(t), load_v(t)
                ce, cw, cn, cs = east(load_c, t), west(load_c, t), north(c), south(c)
                dcx = ce - cw
                dcy = cn - cs
                pe, pw, pn, ps = east(load_p, t), west(load_p, t), north(p), south(p)
                qe, qw, qn, qs = east(load_q, t), west(load_q, t), north(q), south(q)
                mixed[k, t] = (pe - pw) + (qn - qs)
                dst[k, t] = (1.0 - 4.0 * TIME_STEP * DIFFUSION) * c + half * (
                    u * dcx + v * dcy + (2.0 * DIFFUSION) * ((ce + cw) + (cn + cs))
                )
                ue, uw, un, us = east(load_u, t), west(load_u, t), north(u), south(u)
                ve, vw, vn, vs = east(load_v, t), west(load_v, t), north(v), south(v)
                a_e = ue + 2.0 * VISCOSITY
                a_w = 2.0 * VISCOSITY - uw
                a_n = vn + 2.0 * VISCOSITY
                a_s = 2.0 * VISCOSITY - vs
                new_p = keep * p + half * (
                    h * dcx
                    - turn * q
                    - p * (ue - uw)
                    - q * (ve - vw)
                    + (a_e * pe + a_w * pw)
                    + (a_n * pn + a_s * ps)
                )
                new_q = keep * q + half * (
                    h * dcy
                    + turn * p
                    - p * (un - us)
                    - q * (vn - vs)
                    + (a_e * qe + a_w * qw)
                    + (a_n * qn + a_s * qs)
                )
                mask = jnp.where(n == 0, 1.0, read(SEA, t))
                dst[L + k, t] = new_p * mask
                dst[2 * L + k, t] = new_q * mask
            return carry

        lax.fori_loop(0, L, layer_body, 0)
        for t in range(T):
            idx = jnp.concatenate([picked[j, ring(t), :] for j in range(W)], axis=1)
            chosen = jnp.zeros((8, CC), f32)
            for k in range(L):
                chosen = jnp.where(idx == k, src[k, t], chosen)
            acc[t] = acc[t] + TIME_STEP * chosen
            total = mixed[L - 1, t]
            tails = [total]
            for k in range(L - 2, -1, -1):
                total = total + mixed[k, t]
                tails.insert(0, total)
            head = None
            for k in range(L):
                term = (half * gravities[k]) * tails[k]
                head = term if head is None else head + term
                new = dst[k, t] + head
                dst[k, t, :, :COLS] = new[:, :COLS]
                dst[k, t, :, COLS:] = jnp.where(inside, new[:, COLS:], 0.0)

    def two_steps(i, carry):
        one_step(2 * i, cur, nxt)
        one_step(2 * i + 1, nxt, cur)
        return carry

    lax.fori_loop(0, N // 2, two_steps, 0)

    for t in range(T):
        for c in range(CH):
            write(COT + c, t, cur[c, t])
        write(SEA, t, acc[t])


def layer_copies(layer, picked, blocks):
    return [
        (layer.at[row : row + count, lanes(j)], picked.at[j, target : target + count, :])
        for row, target, count in blocks
        for j in range(W - 1)
    ]


def main_kernel(
    early,
    gravities_in,
    states,
    cot,
    sea,
    layer,
    spin,
    edge,
    out,
    forcing,
    planes,
    cur,
    nxt,
    mixed,
    acc,
    picked,
    flags,
    spins,
    edges,
    gravities,
    sems,
    more,
):
    @pl.when(place_of()[3] == early)
    def _():
        blocks = [(0, 0, ROWS)]
        first = start([(gravities_in, gravities), (sea, flags), (edge, edges), (spin, spins)] + layer_copies(layer, picked, blocks), more)
        copies = [own_copies(N, cot, planes, blocks, sems)]
        for n in range(N - 1, -1, -1):
            copies.append(own_copies(n, states.at[n], planes, blocks, sems))
        for group in copies:
            for copy in group:
                copy.start()
        wait(first)
        for j in range(W - 1):
            planes[SEA, j, :ROWS, :] = flags[:, lanes(j)].astype(f32)
        fill_columns(planes, edges, blocks)
        wait(copies[0])
        adjoint_steps(
            ROWS,
            lambda n: wait(own_copies(n, states.at[n], planes, blocks, sems)),
            gravities,
            spins,
            planes,
            picked,
            cur,
            nxt,
            mixed,
            acc,
        )
        pairs = []
        for j in range(W - 1):
            pairs.append((planes.at[COT : COT + CH, j, :ROWS, :], out.at[:, :, lanes(j)]))
            pairs.append((planes.at[SEA, j, :ROWS, :], forcing.at[:, lanes(j)]))
        wait(start(pairs, more))


def early_kernel(gravities, states, cot, sea, layer, spin, edge, west_in, out, forcing, west, *scratch):
    main_kernel(True, gravities, states, cot, sea, layer, spin, edge, out, forcing, *scratch)


def late_kernel(gravities, states, cot, sea, layer, spin, edge, out_in, forcing_in, out, forcing, *scratch):
    main_kernel(False, gravities, states, cot, sea, layer, spin, edge, out, forcing, *scratch)


def rim_kernel(
    gravities_in,
    own,
    sea,
    layer,
    spin,
    from_west,
    from_east,
    edge,
    out_in,
    forcing_in,
    out,
    forcing,
    fields,
    cur,
    nxt,
    mask,
    acc,
    picked,
    flags,
    layers,
    spins,
    tiles,
    gravities,
    more,
):
    first = start([(sea, flags), (layer, layers), (spin, spins), (gravities_in, gravities)], more)
    back = []
    for e, row in enumerate((0, ROWS - 8)):
        back.append((out_in.at[:, row : row + 8, :], tiles.at[e, :CH]))
        back.append((forcing_in.at[row : row + 8, :], tiles.at[e, CH]))
    back = start(back, more.at[4:])

    def put(target, at, q, e, s):
        g, k = divmod(q, 16)
        d = depth(q)
        tile = slice(0, 8) if e == 0 else slice(ROWS - 8, ROWS)
        message = (from_west, from_east)[e]
        here = 4 if e == 0 else 0
        halo = 4 - d if e == 0 else 8
        for j in range(W - 1):
            if q == SEA:
                value = flags[tile, lanes(j)].astype(f32)
            else:
                value = own[e, q // CH, q % CH, :, lanes(j)]
            target[at, j, pl.ds(8 * here + s, 8, stride=8), :] = value
            if d:
                value = message[OFFSET[q] : OFFSET[q] + d, lanes(j)]
                target[at, j, pl.ds(8 * halo + s, d, stride=8), :] = value
        shift = (124 - 8 * k) % 128
        target[at, W - 1, pl.ds(8 * here + s, 8, stride=8), :] = pltpu.roll(edge[g, tile, :], shift, 1)
        corner = pltpu.roll(message[HALO:, lanes(g)], shift, 1)
        target[at, W - 1, pl.ds(8 * (0 if e == 0 else 8) + s, 4, stride=8), :] = corner

    for e in range(2):
        for c in range(CH):
            put(cur, c // L, COT + c, e, 2 * (c % L) + e)
    wait(first)
    for e in range(2):
        for k in range(L):
            put(mask, 0, SEA, e, 2 * k + e)
            for j in range(W - 1):
                tile = slice(0, 4) if e == 0 else slice(ROWS - 4, ROWS)
                picked[j, pl.ds(2 * k + e, 4, stride=8), :] = layers[tile, lanes(j)]

    half = 0.5 * TIME_STEP
    level = lax.broadcasted_iota(jnp.int32, (8, CC), 0) // 2
    sums = []
    for k in range(L):
        sums.append(gravities[k] if k == 0 else sums[-1] + gravities[k])
    couple = []
    for m in range(L):
        weight = jnp.zeros((8, CC), f32)
        for k in range(L):
            weight = jnp.where(level == k, half * sums[min(k, (k - m) % L)], weight)
        couple.append(weight)
    keep = jnp.where(level == L - 1, 1.0 - TIME_STEP * (4.0 * VISCOSITY + BOTTOM_DRAG), 1.0 - TIME_STEP * 4.0 * VISCOSITY)
    place = place_of()
    edge_lane = lax.broadcasted_iota(jnp.int32, (8, 128), 1)
    inside = (edge_lane < 64) & place[1] | (edge_lane >= 64) & place[2]

    def row(ref, at, r):
        return jnp.concatenate([ref[at, j, pl.ds(pl.multiple_of(8 * r, 8), 8), :] for j in range(W)], axis=1)

    def set_row(ref, at, r, value):
        for j in range(W):
            ref[at, j, pl.ds(pl.multiple_of(8 * r, 8), 8), :] = value[:, lanes(j)]

    def north(x):
        return pltpu.roll(x, CC - 1, 1)

    def south(x):
        return pltpu.roll(x, 1, 1)

    for r in range(12):
        sea_r = row(mask, 0, r)
        for at in (1, 2):
            set_row(cur, at, r, row(cur, at, r) * sea_r)
    for r in range(4):
        acc[r] = jnp.zeros((8, COLS), f32)

    for i in range(N):
        n = N - 1 - i
        src, dst = (cur, nxt) if i % 2 == 0 else (nxt, cur)
        for e in range(2):
            for c in range(CH):
                put(fields, c // L, n * CH + c, e, 2 * (c % L) + e)

        for r in range(4):
            idx = jnp.concatenate([picked[j, 8 * r : 8 * r + 8, :] for j in range(W - 1)], axis=1)
            acc[r] = acc[r] + jnp.where(idx == level[:, :COLS], TIME_STEP * row(src, 0, 4 + r)[:, :COLS], 0.0)

        def one_row(r):
            c, p, q = row(src, 0, r), row(src, 1, r), row(src, 2, r)
            h, u, v = row(fields, 0, r), row(fields, 1, r), row(fields, 2, r)
            ce, cw, cn, cs = row(src, 0, r + 1), row(src, 0, r - 1), north(c), south(c)
            pe, pw, pn, ps = row(src, 1, r + 1), row(src, 1, r - 1), north(p), south(p)
            qe, qw, qn, qs = row(src, 2, r + 1), row(src, 2, r - 1), north(q), south(q)
            ue, uw, un, us = row(fields, 1, r + 1), row(fields, 1, r - 1), north(u), south(u)
            ve, vw, vn, vs = row(fields, 2, r + 1), row(fields, 2, r - 1), north(v), south(v)
            dcx = ce - cw
            dcy = cn - cs
            mixed = (pe - pw) + (qn - qs)
            new = (1.0 - 4.0 * TIME_STEP * DIFFUSION) * c + half * (
                u * dcx + v * dcy + (2.0 * DIFFUSION) * ((ce + cw) + (cn + cs))
            )
            for m in range(L):
                new = new + couple[m] * (mixed if m == 0 else pltpu.roll(mixed, 2 * m, 0))
            new = jnp.concatenate([new[:, :COLS], jnp.where(inside, new[:, COLS:], 0.0)], axis=1)
            set_row(dst, 0, r, new)
            a_e = ue + 2.0 * VISCOSITY
            a_w = 2.0 * VISCOSITY - uw
            a_n = vn + 2.0 * VISCOSITY
            a_s = 2.0 * VISCOSITY - vs
            turn = spins[...]
            new_p = keep * p + half * (
                h * dcx
                - turn * q
                - p * (ue - uw)
                - q * (ve - vw)
                + (a_e * pe + a_w * pw)
                + (a_n * pn + a_s * ps)
            )
            new_q = keep * q + half * (
                h * dcy
                + turn * p
                - p * (un - us)
                - q * (vn - vs)
                + (a_e * qe + a_w * qw)
                + (a_n * qn + a_s * qs)
            )
            if n:
                sea_r = row(mask, 0, r)
                new_p, new_q = new_p * sea_r, new_q * sea_r
            set_row(dst, 1, r, new_p)
            set_row(dst, 2, r, new_q)

        def rows_body(b, carry):
            one_row(1 + i + 2 * b)
            one_row(2 + i + 2 * b)
            return carry

        lax.fori_loop(0, 5 - i, rows_body, 0)

    wait(back)
    pairs = []
    for e, start_row in enumerate((0, ROWS - 8)):
        part = slice(0, 4) if e == 0 else slice(4, 8)
        for c in range(CH):
            for j in range(W - 1):
                tiles[e, c, part, lanes(j)] = cur[c // L, j, pl.ds(32 + 2 * (c % L) + e, 4, stride=8), :]
        pairs.append((tiles.at[e, :CH], out.at[:, start_row : start_row + 8, :]))
    copies = start(pairs, more)
    pairs = []
    for e, start_row in enumerate((0, ROWS - 8)):
        for r in range(4):
            total = acc[r]
            total = total + pltpu.roll(total, 4, 0)
            total = total + pltpu.roll(total, 2, 0)
            at = r if e == 0 else 4 + r
            tiles[e, CH, at : at + 1, :] = total[e : e + 1, :]
        pairs.append((tiles.at[e, CH], forcing.at[start_row : start_row + 8, :]))
    copies = copies + start(pairs, more.at[2:])
    wait(copies)


VMEM = pl.BlockSpec(memory_space=pltpu.VMEM)
ANY = pl.BlockSpec(memory_space=pl.ANY)
HBM = pl.BlockSpec(memory_space=pltpu.HBM)
DMA = pltpu.SemaphoreType.DMA
shape = jax.ShapeDtypeStruct


def ring_scratch(rows):
    T = rows // 8
    return [
        pltpu.VMEM((PLANES, W, rows, 128), f32),
        pltpu.VMEM((CH, T, 8, CC), f32),
        pltpu.VMEM((CH, T, 8, CC), f32),
        pltpu.VMEM((L, T, 8, CC), f32),
        pltpu.VMEM((T, 8, CC), f32),
        pltpu.VMEM((W, rows, 128), jnp.int32),
        pltpu.VMEM((ROWS, COLS), jnp.int32),
        pltpu.VMEM((8, CC), f32),
        pltpu.VMEM((GROUPS, ROWS, 128), f32),
    ]


def per_device(saved_states, final_cotangent, gravities, sea_mask, layer_index):
    lons, lats = lax.axis_size("lon"), lax.axis_size("lat")
    lat = lax.axis_index("lat")
    lane = jnp.arange(CC, dtype=jnp.int32)
    lane = jnp.where(lane < COLS + 64, lane, lane - CC)
    lat_rows = (lat * COLS + lane).astype(f32)
    spin = 2.0 * jnp.sin(jnp.pi * ((lat_rows + 0.5) / (lats * COLS) - 0.5))
    spin = jnp.broadcast_to(spin[None], (8, CC))
    strips = pl.pallas_call(
        strip_pack_kernel,
        out_shape=shape((GROUPS, ROWS, 128), f32),
        in_specs=[HBM] * 3,
        out_specs=VMEM,
        scratch_shapes=[
            pltpu.VMEM((N + 1, CH, ROWS, 128), f32),
            pltpu.VMEM((N + 1, CH, ROWS, 128), f32),
            pltpu.VMEM((ROWS, COLS), jnp.int32),
            DMA((5,)),
        ],
        compiler_params=pltpu.CompilerParams(vmem_limit_bytes=60 << 20),
    )(saved_states, final_cotangent, sea_mask)

    def at(i, j):
        return (i % lons) * lats + j

    def swap(x, first):
        pairs = [(at(i, j), at(i, j + 1)) for i in range(lons) for j in range(first, lats - 1, 2)]
        return lax.ppermute(x, ("lon", "lat"), pairs + [(b, a) for a, b in pairs])

    def shift(x, by):
        return lax.ppermute(x, "lon", [(i, (i + by) % lons) for i in range(lons)])

    pair, middle = swap(strips, 0), swap(strips, 1)
    east, west, own = pl.pallas_call(
        row_pack_kernel,
        out_shape=[shape((MESSAGE, COLS), f32)] * 2 + [shape((2, N + 1, CH, 8, COLS), f32)],
        in_specs=[HBM] * 2,
        out_specs=[VMEM] * 3,
        scratch_shapes=[DMA((4,))],
        compiler_params=pltpu.CompilerParams(vmem_limit_bytes=51 << 20),
    )(saved_states, final_cotangent)
    edge, east, west = pl.pallas_call(
        attach_kernel,
        out_shape=[shape((GROUPS, ROWS, 128), f32)] + [shape((MESSAGE, COLS), f32)] * 2,
        in_specs=[HBM, VMEM, VMEM, HBM, HBM],
        out_specs=[VMEM, HBM, HBM],
        scratch_shapes=[pltpu.VMEM((ROWS, COLS), jnp.int32), pltpu.VMEM((2, 8, COLS), f32), DMA((2,))],
        input_output_aliases={3: 1, 4: 2},
        compiler_params=pltpu.CompilerParams(vmem_limit_bytes=51 << 20),
    )(sea_mask, pair, middle, east, west)

    outs = [shape((CH, ROWS, COLS), f32), shape((ROWS, COLS), f32)]
    main = dict(
        scratch_shapes=ring_scratch(ROWS) + [pltpu.SMEM((L,), f32), DMA((N + 1, W - 1, 1)), DMA((16,))],
        compiler_params=pltpu.CompilerParams(vmem_limit_bytes=51 << 20),
        cost_estimate=pl.CostEstimate(flops=160_000_000, bytes_accessed=24_000_000, transcendentals=0),
    )
    fixed = (gravities, saved_states, final_cotangent, sea_mask, layer_index, spin, edge)
    specs = [ANY] + [HBM] * 4 + [ANY] * 2
    from_west = shift(east, 1)
    out, forcing, west = pl.pallas_call(
        early_kernel,
        out_shape=outs + [shape((MESSAGE, COLS), f32)],
        in_specs=specs + [HBM],
        out_specs=[HBM] * 3,
        input_output_aliases={7: 2},
        **main,
    )(*fixed, west)
    from_east = shift(west, -1)
    out, forcing = pl.pallas_call(
        late_kernel,
        out_shape=outs,
        in_specs=specs + [HBM] * 2,
        out_specs=[HBM] * 2,
        input_output_aliases={7: 0, 8: 1},
        **main,
    )(*fixed, out, forcing)

    return pl.pallas_call(
        rim_kernel,
        out_shape=outs,
        in_specs=[ANY, VMEM, ANY, ANY, ANY] + [VMEM] * 3 + [HBM] * 2,
        out_specs=[HBM, HBM],
        scratch_shapes=[
            pltpu.VMEM((3, W, 96, 128), f32),
            pltpu.VMEM((3, W, 96, 128), f32),
            pltpu.VMEM((3, W, 96, 128), f32),
            pltpu.VMEM((1, W, 96, 128), f32),
            pltpu.VMEM((4, 8, COLS), f32),
            pltpu.VMEM((W - 1, 32, 128), jnp.int32),
            pltpu.VMEM((ROWS, COLS), jnp.int32),
            pltpu.VMEM((ROWS, COLS), jnp.int32),
            pltpu.VMEM((8, CC), f32),
            pltpu.VMEM((2, CH + 1, 8, COLS), f32),
            pltpu.SMEM((L,), f32),
            DMA((8,)),
        ],
        input_output_aliases={8: 0, 9: 1},
        compiler_params=pltpu.CompilerParams(vmem_limit_bytes=51 << 20),
    )(
        gravities,
        own,
        sea_mask,
        layer_index,
        spin,
        from_west,
        from_east,
        edge,
        out,
        forcing,
    )


def solution(mesh):
    return jax.shard_map(
        per_device,
        mesh=mesh,
        in_specs=(
            P(None, None, "lon", "lat"),
            P(None, "lon", "lat"),
            P(),
            P("lon", "lat"),
            P("lon", "lat"),
        ),
        out_specs=(P(None, "lon", "lat"), P("lon", "lat")),
        check_vma=False,
    )
```

```python
import jax
import jax.numpy as jnp
from jax import lax
from jax.experimental import pallas as pl
from jax.experimental.pallas import tpu as pltpu
from jax.sharding import PartitionSpec as P

TIME_STEP = 0.3
VISCOSITY = 0.1
DIFFUSION = 0.05
BOTTOM_DRAG = 0.2

L = 4
N = 4
CH = 3 * L
ROWS = 32
COLS = 512
CC = COLS + 128
W = CC // 128

COT = N * CH
SEA = COT + CH
PLANES = SEA + 1
GROUPS = -(-PLANES // 16)
f32 = jnp.float32


def place_of():
    lon, lat = lax.axis_index("lon"), lax.axis_index("lat")
    return lat % 2, lat < lax.axis_size("lat") - 1, lat > 0, lon == 0


def lanes(j):
    return slice(128 * j, 128 * j + 128)


def depth(q):
    if q >= COT:
        return N
    n, c = divmod(q, CH)
    return n + 1 if c >= L else n


OFFSET = {}
HALO = 0
for _q in sorted(range(SEA), key=lambda q: -depth(q)) + [SEA]:
    if depth(_q):
        OFFSET[_q] = HALO
        HALO += depth(_q)
MESSAGE = HALO + N
TAIL = MESSAGE - 8
assert OFFSET[SEA] == TAIL


def start(pairs, sems):
    copies = [pltpu.make_async_copy(a, b, sems.at[i]) for i, (a, b) in enumerate(pairs)]
    for copy in copies:
        copy.start()
    return copies


def wait(copies):
    for copy in copies:
        copy.wait()


def strip_pack_kernel(states, cot, sea, strips, left, right, flags, sems):
    copies = []
    for n in range(N + 1):
        source = cot if n == N else states.at[n]
        pairs = [
            (source.at[:, :, slice(0, 128)], left.at[n]),
            (source.at[:, :, slice(COLS - 128, COLS)], right.at[n]),
        ]
        copies.append(start(pairs, sems.at[n]))
    copies[N].extend(start([(sea, flags)], sems.at[N + 1]))
    lane = lax.broadcasted_iota(jnp.int32, (ROWS, 128), 1)
    for g in range(GROUPS):
        total = jnp.zeros((ROWS, 128), f32)
        while copies and (N + 1 - len(copies)) * CH < g * 16 + 16:
            wait(copies.pop(0))
        for k in range(16):
            q = g * 16 + k
            if q >= PLANES:
                continue
            if q == SEA:
                first, last = flags[:, lanes(0)].astype(f32), flags[:, lanes(W - 2)].astype(f32)
            else:
                first, last = left[q // CH, q % CH], right[q // CH, q % CH]
            both = pltpu.roll(jnp.where(lane >= 124, last, first), (8 * k + 4) % 128, 1)
            total = jnp.where(lane // 8 == k, both, total)
        strips[g] = total


def row_pack_kernel(states, cot, east, west, own, sems):
    pairs = []
    for e, rows in enumerate((slice(0, 8), slice(ROWS - 8, ROWS))):
        pairs.append((states.at[:, :, rows, :], own.at[e, :N]))
        pairs.append((cot.at[:, rows, :], own.at[e, N]))
    wait(start(pairs, sems))
    for q, row in OFFSET.items():
        if q == SEA:
            continue
        d = depth(q)
        east[row : row + d] = own[1, q // CH, q % CH, 8 - d :]
        west[row : row + d] = own[0, q // CH, q % CH, :d]


def attach_kernel(sea, pair, middle, east_in, west_in, edge, east, west, flags, tails, sems):
    copies = start([(sea, flags)], sems)
    odd = place_of()[0] == 1
    south = lax.broadcasted_iota(jnp.int32, (ROWS, 128), 1) % 8 < 4
    for g in range(GROUPS):
        merged = jnp.where(south == odd, pair[g], middle[g])
        edge[g] = merged
        tails[0, N:, lanes(g)] = merged[ROWS - N :]
        tails[1, N:, lanes(g)] = merged[:N]
    wait(copies)
    tails[0, :N, :] = flags[ROWS - N :].astype(f32)
    tails[1, :N, :] = flags[:N].astype(f32)
    wait(start([(tails.at[0], east.at[TAIL:, :]), (tails.at[1], west.at[TAIL:, :])], sems))


def fill_columns(planes, edge, blocks):
    for source, target, count in blocks:
        for q in range(PLANES):
            g, k = divmod(q, 16)
            planes[q, W - 1, target : target + count, :] = pltpu.roll(
                edge[g, source : source + count, :], (124 - 8 * k) % 128, 1
            )


def own_copies(n, source, planes, blocks, sems):
    return [
        pltpu.make_async_copy(
            source.at[:, row : row + count, lanes(j)],
            planes.at[pl.ds(n * CH, CH), j, target : target + count, :],
            sems.at[n, j, i],
        )
        for i, (row, target, count) in enumerate(blocks)
        for j in range(W - 1)
    ]


def adjoint_steps(rows, arrive, gravities, spin, planes, picked, cur, nxt, mixed, acc):
    T = rows // 8
    half = 0.5 * TIME_STEP

    def ring(t):
        return pl.ds(t, 8, stride=T)

    def read(q, t):
        return jnp.concatenate([planes[q, j, ring(t), :] for j in range(W)], axis=1)

    def write(q, t, value):
        for j in range(W - 1):
            planes[q, j, ring(t), :] = value[:, lanes(j)]

    for t in range(T):
        sea_t = read(SEA, t)
        for c in range(CH):
            value = read(COT + c, t)
            cur[c, t] = value if c < L else value * sea_t
        acc[t] = jnp.zeros((8, CC), f32)

    place = place_of()
    edge_lane = lax.broadcasted_iota(jnp.int32, (8, 128), 1)
    inside = (edge_lane < 64) & place[1] | (edge_lane >= 64) & place[2]

    def north(x):
        return pltpu.roll(x, CC - 1, 1)

    def south(x):
        return pltpu.roll(x, 1, 1)

    def east(load, t):
        return load(t + 1) if t + 1 < T else pltpu.roll(load(0), 7, 0)

    def west(load, t):
        return load(t - 1) if t > 0 else pltpu.roll(load(T - 1), 1, 0)

    def one_step(index, src, dst):
        n = N - 1 - index
        arrive(n)

        def layer_body(k, carry):
            load_h = lambda t: read(n * CH + k, t)
            load_u = lambda t: read(n * CH + L + k, t)
            load_v = lambda t: read(n * CH + 2 * L + k, t)
            load_c = lambda t: src[k, t]
            load_p = lambda t: src[L + k, t]
            load_q = lambda t: src[2 * L + k, t]
            drag = jnp.where(k == L - 1, BOTTOM_DRAG, 0.0)
            keep = 1.0 - TIME_STEP * (4.0 * VISCOSITY + drag)
            turn = spin[...]
            for t in range(T):
                c, p, q = load_c(t), load_p(t), load_q(t)
                h, u, v = load_h(t), load_u(t), load_v(t)
                ce, cw, cn, cs = east(load_c, t), west(load_c, t), north(c), south(c)
                dcx = ce - cw
                dcy = cn - cs
                pe, pw, pn, ps = east(load_p, t), west(load_p, t), north(p), south(p)
                qe, qw, qn, qs = east(load_q, t), west(load_q, t), north(q), south(q)
                mixed[k, t] = (pe - pw) + (qn - qs)
                dst[k, t] = (1.0 - 4.0 * TIME_STEP * DIFFUSION) * c + half * (
                    u * dcx + v * dcy + (2.0 * DIFFUSION) * ((ce + cw) + (cn + cs))
                )
                ue, uw, un, us = east(load_u, t), west(load_u, t), north(u), south(u)
                ve, vw, vn, vs = east(load_v, t), west(load_v, t), north(v), south(v)
                a_e = ue + 2.0 * VISCOSITY
                a_w = 2.0 * VISCOSITY - uw
                a_n = vn + 2.0 * VISCOSITY
                a_s = 2.0 * VISCOSITY - vs
                new_p = keep * p + half * (
                    h * dcx
                    - turn * q
                    - p * (ue - uw)
                    - q * (ve - vw)
                    + (a_e * pe + a_w * pw)
                    + (a_n * pn + a_s * ps)
                )
                new_q = keep * q + half * (
                    h * dcy
                    + turn * p
                    - p * (un - us)
                    - q * (vn - vs)
                    + (a_e * qe + a_w * qw)
                    + (a_n * qn + a_s * qs)
                )
                mask = jnp.where(n == 0, 1.0, read(SEA, t))
                dst[L + k, t] = new_p * mask
                dst[2 * L + k, t] = new_q * mask
            return carry

        lax.fori_loop(0, L, layer_body, 0)
        for t in range(T):
            idx = jnp.concatenate([picked[j, ring(t), :] for j in range(W)], axis=1)
            chosen = jnp.zeros((8, CC), f32)
            for k in range(L):
                chosen = jnp.where(idx == k, src[k, t], chosen)
            acc[t] = acc[t] + TIME_STEP * chosen
            total = mixed[L - 1, t]
            tails = [total]
            for k in range(L - 2, -1, -1):
                total = total + mixed[k, t]
                tails.insert(0, total)
            head = None
            for k in range(L):
                term = (half * gravities[k]) * tails[k]
                head = term if head is None else head + term
                new = dst[k, t] + head
                dst[k, t, :, :COLS] = new[:, :COLS]
                dst[k, t, :, COLS:] = jnp.where(inside, new[:, COLS:], 0.0)

    def two_steps(i, carry):
        one_step(2 * i, cur, nxt)
        one_step(2 * i + 1, nxt, cur)
        return carry

    lax.fori_loop(0, N // 2, two_steps, 0)

    for t in range(T):
        for c in range(CH):
            write(COT + c, t, cur[c, t])
        write(SEA, t, acc[t])


def layer_copies(layer, picked, blocks):
    return [
        (layer.at[row : row + count, lanes(j)], picked.at[j, target : target + count, :])
        for row, target, count in blocks
        for j in range(W - 1)
    ]


def main_kernel(
    early,
    gravities_in,
    states,
    cot,
    sea,
    layer,
    spin,
    edge,
    out,
    forcing,
    planes,
    cur,
    nxt,
    mixed,
    acc,
    picked,
    flags,
    spins,
    edges,
    gravities,
    sems,
    more,
):
    @pl.when(place_of()[3] == early)
    def _():
        blocks = [(0, 0, ROWS)]
        first = start([(gravities_in, gravities), (sea, flags), (edge, edges), (spin, spins)] + layer_copies(layer, picked, blocks), more)
        copies = [own_copies(N, cot, planes, blocks, sems)]
        for n in range(N - 1, -1, -1):
            copies.append(own_copies(n, states.at[n], planes, blocks, sems))
        for group in copies:
            for copy in group:
                copy.start()
        wait(first)
        for j in range(W - 1):
            planes[SEA, j, :ROWS, :] = flags[:, lanes(j)].astype(f32)
        fill_columns(planes, edges, blocks)
        wait(copies[0])
        adjoint_steps(
            ROWS,
            lambda n: wait(own_copies(n, states.at[n], planes, blocks, sems)),
            gravities,
            spins,
            planes,
            picked,
            cur,
            nxt,
            mixed,
            acc,
        )
        pairs = []
        for j in range(W - 1):
            pairs.append((planes.at[COT : COT + CH, j, :ROWS, :], out.at[:, :, lanes(j)]))
            pairs.append((planes.at[SEA, j, :ROWS, :], forcing.at[:, lanes(j)]))
        wait(start(pairs, more))


def early_kernel(gravities, states, cot, sea, layer, spin, edge, west_in, out, forcing, west, *scratch):
    main_kernel(True, gravities, states, cot, sea, layer, spin, edge, out, forcing, *scratch)


def late_kernel(gravities, states, cot, sea, layer, spin, edge, out_in, forcing_in, out, forcing, *scratch):
    main_kernel(False, gravities, states, cot, sea, layer, spin, edge, out, forcing, *scratch)


def rim_kernel(
    gravities_in,
    own,
    sea,
    layer,
    spin,
    from_west,
    from_east,
    edge,
    out_in,
    forcing_in,
    out,
    forcing,
    fields,
    cur,
    nxt,
    mask,
    acc,
    picked,
    flags,
    layers,
    spins,
    tiles,
    gravities,
    more,
):
    first = start([(sea, flags), (layer, layers), (spin, spins), (gravities_in, gravities)], more)
    back = []
    for e, row in enumerate((0, ROWS - 8)):
        back.append((out_in.at[:, row : row + 8, :], tiles.at[e, :CH]))
        back.append((forcing_in.at[row : row + 8, :], tiles.at[e, CH]))
    back = start(back, more.at[4:])

    def put(target, at, q, e, s):
        g, k = divmod(q, 16)
        d = depth(q)
        tile = slice(0, 8) if e == 0 else slice(ROWS - 8, ROWS)
        message = (from_west, from_east)[e]
        here = 4 if e == 0 else 0
        halo = 4 - d if e == 0 else 8
        for j in range(W - 1):
            if q == SEA:
                value = flags[tile, lanes(j)].astype(f32)
            else:
                value = own[e, q // CH, q % CH, :, lanes(j)]
            target[at, j, pl.ds(8 * here + s, 8, stride=8), :] = value
            if d:
                value = message[OFFSET[q] : OFFSET[q] + d, lanes(j)]
                target[at, j, pl.ds(8 * halo + s, d, stride=8), :] = value
        shift = (124 - 8 * k) % 128
        target[at, W - 1, pl.ds(8 * here + s, 8, stride=8), :] = pltpu.roll(edge[g, tile, :], shift, 1)
        corner = pltpu.roll(message[HALO:, lanes(g)], shift, 1)
        target[at, W - 1, pl.ds(8 * (0 if e == 0 else 8) + s, 4, stride=8), :] = corner

    for e in range(2):
        for c in range(CH):
            put(cur, c // L, COT + c, e, 2 * (c % L) + e)
    wait(first)
    for e in range(2):
        for k in range(L):
            put(mask, 0, SEA, e, 2 * k + e)
            for j in range(W - 1):
                tile = slice(0, 4) if e == 0 else slice(ROWS - 4, ROWS)
                picked[j, pl.ds(2 * k + e, 4, stride=8), :] = layers[tile, lanes(j)]

    half = 0.5 * TIME_STEP
    level = lax.broadcasted_iota(jnp.int32, (8, CC), 0) // 2
    sums = []
    for k in range(L):
        sums.append(gravities[k] if k == 0 else sums[-1] + gravities[k])
    couple = []
    for m in range(L):
        weight = jnp.zeros((8, CC), f32)
        for k in range(L):
            weight = jnp.where(level == k, half * sums[min(k, (k - m) % L)], weight)
        couple.append(weight)
    keep = jnp.where(level == L - 1, 1.0 - TIME_STEP * (4.0 * VISCOSITY + BOTTOM_DRAG), 1.0 - TIME_STEP * 4.0 * VISCOSITY)
    place = place_of()
    edge_lane = lax.broadcasted_iota(jnp.int32, (8, 128), 1)
    inside = (edge_lane < 64) & place[1] | (edge_lane >= 64) & place[2]

    def row(ref, at, r):
        return jnp.concatenate([ref[at, j, pl.ds(pl.multiple_of(8 * r, 8), 8), :] for j in range(W)], axis=1)

    def set_row(ref, at, r, value):
        for j in range(W):
            ref[at, j, pl.ds(pl.multiple_of(8 * r, 8), 8), :] = value[:, lanes(j)]

    def north(x):
        return pltpu.roll(x, CC - 1, 1)

    def south(x):
        return pltpu.roll(x, 1, 1)

    for r in range(12):
        sea_r = row(mask, 0, r)
        for at in (1, 2):
            set_row(cur, at, r, row(cur, at, r) * sea_r)
    for r in range(4):
        acc[r] = jnp.zeros((8, COLS), f32)

    for i in range(N):
        n = N - 1 - i
        src, dst = (cur, nxt) if i % 2 == 0 else (nxt, cur)
        for e in range(2):
            for c in range(CH):
                put(fields, c // L, n * CH + c, e, 2 * (c % L) + e)

        for r in range(4):
            idx = jnp.concatenate([picked[j, 8 * r : 8 * r + 8, :] for j in range(W - 1)], axis=1)
            acc[r] = acc[r] + jnp.where(idx == level[:, :COLS], TIME_STEP * row(src, 0, 4 + r)[:, :COLS], 0.0)

        def one_row(r):
            c, p, q = row(src, 0, r), row(src, 1, r), row(src, 2, r)
            h, u, v = row(fields, 0, r), row(fields, 1, r), row(fields, 2, r)
            ce, cw, cn, cs = row(src, 0, r + 1), row(src, 0, r - 1), north(c), south(c)
            pe, pw, pn, ps = row(src, 1, r + 1), row(src, 1, r - 1), north(p), south(p)
            qe, qw, qn, qs = row(src, 2, r + 1), row(src, 2, r - 1), north(q), south(q)
            ue, uw, un, us = row(fields, 1, r + 1), row(fields, 1, r - 1), north(u), south(u)
            ve, vw, vn, vs = row(fields, 2, r + 1), row(fields, 2, r - 1), north(v), south(v)
            dcx = ce - cw
            dcy = cn - cs
            mixed = (pe - pw) + (qn - qs)
            new = (1.0 - 4.0 * TIME_STEP * DIFFUSION) * c + half * (
                u * dcx + v * dcy + (2.0 * DIFFUSION) * ((ce + cw) + (cn + cs))
            )
            for m in range(L):
                new = new + couple[m] * (mixed if m == 0 else pltpu.roll(mixed, 2 * m, 0))
            new = jnp.concatenate([new[:, :COLS], jnp.where(inside, new[:, COLS:], 0.0)], axis=1)
            set_row(dst, 0, r, new)
            a_e = ue + 2.0 * VISCOSITY
            a_w = 2.0 * VISCOSITY - uw
            a_n = vn + 2.0 * VISCOSITY
            a_s = 2.0 * VISCOSITY - vs
            turn = spins[...]
            new_p = keep * p + half * (
                h * dcx
                - turn * q
                - p * (ue - uw)
                - q * (ve - vw)
                + (a_e * pe + a_w * pw)
                + (a_n * pn + a_s * ps)
            )
            new_q = keep * q + half * (
                h * dcy
                + turn * p
                - p * (un - us)
                - q * (vn - vs)
                + (a_e * qe + a_w * qw)
                + (a_n * qn + a_s * qs)
            )
            if n:
                sea_r = row(mask, 0, r)
                new_p, new_q = new_p * sea_r, new_q * sea_r
            set_row(dst, 1, r, new_p)
            set_row(dst, 2, r, new_q)

        def rows_body(b, carry):
            one_row(1 + i + 2 * b)
            one_row(2 + i + 2 * b)
            return carry

        lax.fori_loop(0, 5 - i, rows_body, 0)

    wait(back)
    pairs = []
    for e, start_row in enumerate((0, ROWS - 8)):
        part = slice(0, 4) if e == 0 else slice(4, 8)
        for c in range(CH):
            for j in range(W - 1):
                tiles[e, c, part, lanes(j)] = cur[c // L, j, pl.ds(32 + 2 * (c % L) + e, 4, stride=8), :]
        pairs.append((tiles.at[e, :CH], out.at[:, start_row : start_row + 8, :]))
    copies = start(pairs, more)
    pairs = []
    for e, start_row in enumerate((0, ROWS - 8)):
        for r in range(4):
            total = acc[r]
            total = total + pltpu.roll(total, 4, 0)
            total = total + pltpu.roll(total, 2, 0)
            at = r if e == 0 else 4 + r
            tiles[e, CH, at : at + 1, :] = total[e : e + 1, :]
        pairs.append((tiles.at[e, CH], forcing.at[start_row : start_row + 8, :]))
    copies = copies + start(pairs, more.at[2:])
    wait(copies)


VMEM = pl.BlockSpec(memory_space=pltpu.VMEM)
ANY = pl.BlockSpec(memory_space=pl.ANY)
HBM = pl.BlockSpec(memory_space=pltpu.HBM)
DMA = pltpu.SemaphoreType.DMA
shape = jax.ShapeDtypeStruct


def ring_scratch(rows):
    T = rows // 8
    return [
        pltpu.VMEM((PLANES, W, rows, 128), f32),
        pltpu.VMEM((CH, T, 8, CC), f32),
        pltpu.VMEM((CH, T, 8, CC), f32),
        pltpu.VMEM((L, T, 8, CC), f32),
        pltpu.VMEM((T, 8, CC), f32),
        pltpu.VMEM((W, rows, 128), jnp.int32),
        pltpu.VMEM((ROWS, COLS), jnp.int32),
        pltpu.VMEM((8, CC), f32),
        pltpu.VMEM((GROUPS, ROWS, 128), f32),
    ]


def per_device(saved_states, final_cotangent, gravities, sea_mask, layer_index):
    lons, lats = lax.axis_size("lon"), lax.axis_size("lat")
    lat = lax.axis_index("lat")
    lane = jnp.arange(CC, dtype=jnp.int32)
    lane = jnp.where(lane < COLS + 64, lane, lane - CC)
    lat_rows = (lat * COLS + lane).astype(f32)
    spin = 2.0 * jnp.sin(jnp.pi * ((lat_rows + 0.5) / (lats * COLS) - 0.5))
    spin = jnp.broadcast_to(spin[None], (8, CC))
    strips = pl.pallas_call(
        strip_pack_kernel,
        out_shape=shape((GROUPS, ROWS, 128), f32),
        in_specs=[HBM] * 3,
        out_specs=VMEM,
        scratch_shapes=[
            pltpu.VMEM((N + 1, CH, ROWS, 128), f32),
            pltpu.VMEM((N + 1, CH, ROWS, 128), f32),
            pltpu.VMEM((ROWS, COLS), jnp.int32),
            DMA((N + 2, 2)),
        ],
        compiler_params=pltpu.CompilerParams(vmem_limit_bytes=60 << 20),
    )(saved_states, final_cotangent, sea_mask)

    def at(i, j):
        return (i % lons) * lats + j

    def swap(x, first):
        pairs = [(at(i, j), at(i, j + 1)) for i in range(lons) for j in range(first, lats - 1, 2)]
        return lax.ppermute(x, ("lon", "lat"), pairs + [(b, a) for a, b in pairs])

    def shift(x, by):
        return lax.ppermute(x, "lon", [(i, (i + by) % lons) for i in range(lons)])

    pair, middle = swap(strips, 0), swap(strips, 1)
    east, west, own = pl.pallas_call(
        row_pack_kernel,
        out_shape=[shape((MESSAGE, COLS), f32)] * 2 + [shape((2, N + 1, CH, 8, COLS), f32)],
        in_specs=[HBM] * 2,
        out_specs=[VMEM] * 3,
        scratch_shapes=[DMA((4,))],
        compiler_params=pltpu.CompilerParams(vmem_limit_bytes=51 << 20),
    )(saved_states, final_cotangent)
    edge, east, west = pl.pallas_call(
        attach_kernel,
        out_shape=[shape((GROUPS, ROWS, 128), f32)] + [shape((MESSAGE, COLS), f32)] * 2,
        in_specs=[HBM, VMEM, VMEM, HBM, HBM],
        out_specs=[VMEM, HBM, HBM],
        scratch_shapes=[pltpu.VMEM((ROWS, COLS), jnp.int32), pltpu.VMEM((2, 8, COLS), f32), DMA((2,))],
        input_output_aliases={3: 1, 4: 2},
        compiler_params=pltpu.CompilerParams(vmem_limit_bytes=51 << 20),
    )(sea_mask, pair, middle, east, west)

    outs = [shape((CH, ROWS, COLS), f32), shape((ROWS, COLS), f32)]
    main = dict(
        scratch_shapes=ring_scratch(ROWS) + [pltpu.SMEM((L,), f32), DMA((N + 1, W - 1, 1)), DMA((16,))],
        compiler_params=pltpu.CompilerParams(vmem_limit_bytes=51 << 20),
        cost_estimate=pl.CostEstimate(flops=160_000_000, bytes_accessed=24_000_000, transcendentals=0),
    )
    fixed = (gravities, saved_states, final_cotangent, sea_mask, layer_index, spin, edge)
    specs = [ANY] + [HBM] * 4 + [ANY] * 2
    from_west = shift(east, 1)
    out, forcing, west = pl.pallas_call(
        early_kernel,
        out_shape=outs + [shape((MESSAGE, COLS), f32)],
        in_specs=specs + [HBM],
        out_specs=[HBM] * 3,
        input_output_aliases={7: 2},
        **main,
    )(*fixed, west)
    from_east = shift(west, -1)
    out, forcing = pl.pallas_call(
        late_kernel,
        out_shape=outs,
        in_specs=specs + [HBM] * 2,
        out_specs=[HBM] * 2,
        input_output_aliases={7: 0, 8: 1},
        **main,
    )(*fixed, out, forcing)

    return pl.pallas_call(
        rim_kernel,
        out_shape=outs,
        in_specs=[ANY, VMEM, ANY, ANY, ANY] + [VMEM] * 3 + [HBM] * 2,
        out_specs=[HBM, HBM],
        scratch_shapes=[
            pltpu.VMEM((3, W, 96, 128), f32),
            pltpu.VMEM((3, W, 96, 128), f32),
            pltpu.VMEM((3, W, 96, 128), f32),
            pltpu.VMEM((1, W, 96, 128), f32),
            pltpu.VMEM((4, 8, COLS), f32),
            pltpu.VMEM((W - 1, 32, 128), jnp.int32),
            pltpu.VMEM((ROWS, COLS), jnp.int32),
            pltpu.VMEM((ROWS, COLS), jnp.int32),
            pltpu.VMEM((8, CC), f32),
            pltpu.VMEM((2, CH + 1, 8, COLS), f32),
            pltpu.SMEM((L,), f32),
            DMA((8,)),
        ],
        input_output_aliases={8: 0, 9: 1},
        compiler_params=pltpu.CompilerParams(vmem_limit_bytes=51 << 20),
    )(
        gravities,
        own,
        sea_mask,
        layer_index,
        spin,
        from_west,
        from_east,
        edge,
        out,
        forcing,
    )


def solution(mesh):
    return jax.shard_map(
        per_device,
        mesh=mesh,
        in_specs=(
            P(None, None, "lon", "lat"),
            P(None, "lon", "lat"),
            P(),
            P("lon", "lat"),
            P("lon", "lat"),
        ),
        out_specs=(P(None, "lon", "lat"), P("lon", "lat")),
        check_vma=False,
    )
```

```python
import jax
import jax.numpy as jnp
from jax import lax
from jax.experimental import pallas as pl
from jax.experimental.pallas import tpu as pltpu
from jax.sharding import PartitionSpec as P

TIME_STEP = 0.3
VISCOSITY = 0.1
DIFFUSION = 0.05
BOTTOM_DRAG = 0.2

L = 4
N = 4
CH = 3 * L
ROWS = 32
COLS = 512
CC = COLS + 128
W = CC // 128

COT = N * CH
SEA = COT + CH
PLANES = SEA + 1
GROUPS = -(-PLANES // 16)
f32 = jnp.float32


def place_of():
    lon, lat = lax.axis_index("lon"), lax.axis_index("lat")
    return lat % 2, lat < lax.axis_size("lat") - 1, lat > 0, lon == 0


def lanes(j):
    return slice(128 * j, 128 * j + 128)


def depth(q):
    if q >= COT:
        return N
    n, c = divmod(q, CH)
    return n + 1 if c >= L else n


OFFSET = {}
HALO = 0
for _q in sorted(range(SEA), key=lambda q: -depth(q)) + [SEA]:
    if depth(_q):
        OFFSET[_q] = HALO
        HALO += depth(_q)
MESSAGE = HALO + N
TAIL = MESSAGE - 8
assert OFFSET[SEA] == TAIL


def start(pairs, sems):
    copies = [pltpu.make_async_copy(a, b, sems.at[i]) for i, (a, b) in enumerate(pairs)]
    for copy in copies:
        copy.start()
    return copies


def wait(copies):
    for copy in copies:
        copy.wait()


def strip_pack_kernel(states, cot, sea, strips, left, right, flags, sems):
    copies = []
    for n in range(N + 1):
        source = cot if n == N else states.at[n]
        pairs = [
            (source.at[:, :, slice(0, 128)], left.at[n]),
            (source.at[:, :, slice(COLS - 128, COLS)], right.at[n]),
        ]
        copies.append(start(pairs, sems.at[n]))
    copies[N].extend(start([(sea, flags)], sems.at[N + 1]))
    lane = lax.broadcasted_iota(jnp.int32, (ROWS, 128), 1)
    for g in range(GROUPS):
        total = jnp.zeros((ROWS, 128), f32)
        while copies and (N + 1 - len(copies)) * CH < g * 16 + 16:
            wait(copies.pop(0))
        for k in range(16):
            q = g * 16 + k
            if q >= PLANES:
                continue
            if q == SEA:
                first, last = flags[:, lanes(0)].astype(f32), flags[:, lanes(W - 2)].astype(f32)
            else:
                first, last = left[q // CH, q % CH], right[q // CH, q % CH]
            both = pltpu.roll(jnp.where(lane >= 124, last, first), (8 * k + 4) % 128, 1)
            total = jnp.where(lane // 8 == k, both, total)
        strips[g] = total


def row_pack_kernel(states, cot, east, west, own, sems):
    pairs = []
    for e, rows in enumerate((slice(0, 8), slice(ROWS - 8, ROWS))):
        pairs.append((states.at[:, :, rows, :], own.at[e, :N]))
        pairs.append((cot.at[:, rows, :], own.at[e, N]))
    wait(start(pairs, sems))
    for q, row in OFFSET.items():
        if q == SEA:
            continue
        d = depth(q)
        east[row : row + d] = own[1, q // CH, q % CH, 8 - d :]
        west[row : row + d] = own[0, q // CH, q % CH, :d]


def attach_kernel(sea, pair, middle, east_in, west_in, edge, east, west, flags, tails, sems):
    copies = start([(sea, flags)], sems)
    odd = place_of()[0] == 1
    south = lax.broadcasted_iota(jnp.int32, (ROWS, 128), 1) % 8 < 4
    for g in range(GROUPS):
        merged = jnp.where(south == odd, pair[g], middle[g])
        edge[g] = merged
        tails[0, N:, lanes(g)] = merged[ROWS - N :]
        tails[1, N:, lanes(g)] = merged[:N]
    wait(copies)
    tails[0, :N, :] = flags[ROWS - N :].astype(f32)
    tails[1, :N, :] = flags[:N].astype(f32)
    wait(start([(tails.at[0], east.at[TAIL:, :]), (tails.at[1], west.at[TAIL:, :])], sems))


def fill_columns(planes, edge, blocks):
    for source, target, count in blocks:
        for q in range(PLANES):
            g, k = divmod(q, 16)
            planes[q, W - 1, target : target + count, :] = pltpu.roll(
                edge[g, source : source + count, :], (124 - 8 * k) % 128, 1
            )


def own_copies(n, source, planes, blocks, sems):
    return [
        pltpu.make_async_copy(
            source.at[:, row : row + count, lanes(j)],
            planes.at[pl.ds(n * CH, CH), j, target : target + count, :],
            sems.at[n, j, i],
        )
        for i, (row, target, count) in enumerate(blocks)
        for j in range(W - 1)
    ]


def adjoint_steps(rows, arrive, gravities, spin, planes, picked, cur, nxt, mixed, acc):
    T = rows // 8
    half = 0.5 * TIME_STEP

    def ring(t):
        return pl.ds(t, 8, stride=T)

    def read(q, t):
        return jnp.concatenate([planes[q, j, ring(t), :] for j in range(W)], axis=1)

    def write(q, t, value):
        for j in range(W - 1):
            planes[q, j, ring(t), :] = value[:, lanes(j)]

    for t in range(T):
        sea_t = read(SEA, t)
        for c in range(CH):
            value = read(COT + c, t)
            cur[c, t] = value if c < L else value * sea_t
        acc[t] = jnp.zeros((8, CC), f32)

    place = place_of()
    edge_lane = lax.broadcasted_iota(jnp.int32, (8, 128), 1)
    inside = (edge_lane < 64) & place[1] | (edge_lane >= 64) & place[2]

    def north(x):
        return pltpu.roll(x, CC - 1, 1)

    def south(x):
        return pltpu.roll(x, 1, 1)

    def east(load, t):
        return load(t + 1) if t + 1 < T else pltpu.roll(load(0), 7, 0)

    def west(load, t):
        return load(t - 1) if t > 0 else pltpu.roll(load(T - 1), 1, 0)

    def one_step(index, src, dst):
        n = N - 1 - index
        arrive(n)

        def layer_body(k, carry):
            load_h = lambda t: read(n * CH + k, t)
            load_u = lambda t: read(n * CH + L + k, t)
            load_v = lambda t: read(n * CH + 2 * L + k, t)
            load_c = lambda t: src[k, t]
            load_p = lambda t: src[L + k, t]
            load_q = lambda t: src[2 * L + k, t]
            drag = jnp.where(k == L - 1, BOTTOM_DRAG, 0.0)
            keep = 1.0 - TIME_STEP * (4.0 * VISCOSITY + drag)
            turn = spin[...]
            for t in range(T):
                c, p, q = load_c(t), load_p(t), load_q(t)
                h, u, v = load_h(t), load_u(t), load_v(t)
                ce, cw, cn, cs = east(load_c, t), west(load_c, t), north(c), south(c)
                dcx = ce - cw
                dcy = cn - cs
                pe, pw, pn, ps = east(load_p, t), west(load_p, t), north(p), south(p)
                qe, qw, qn, qs = east(load_q, t), west(load_q, t), north(q), south(q)
                mixed[k, t] = (pe - pw) + (qn - qs)
                dst[k, t] = (1.0 - 4.0 * TIME_STEP * DIFFUSION) * c + half * (
                    u * dcx + v * dcy + (2.0 * DIFFUSION) * ((ce + cw) + (cn + cs))
                )
                ue, uw, un, us = east(load_u, t), west(load_u, t), north(u), south(u)
                ve, vw, vn, vs = east(load_v, t), west(load_v, t), north(v), south(v)
                a_e = ue + 2.0 * VISCOSITY
                a_w = 2.0 * VISCOSITY - uw
                a_n = vn + 2.0 * VISCOSITY
                a_s = 2.0 * VISCOSITY - vs
                new_p = keep * p + half * (
                    h * dcx
                    - turn * q
                    - p * (ue - uw)
                    - q * (ve - vw)
                    + (a_e * pe + a_w * pw)
                    + (a_n * pn + a_s * ps)
                )
                new_q = keep * q + half * (
                    h * dcy
                    + turn * p
                    - p * (un - us)
                    - q * (vn - vs)
                    + (a_e * qe + a_w * qw)
                    + (a_n * qn + a_s * qs)
                )
                mask = jnp.where(n == 0, 1.0, read(SEA, t))
                dst[L + k, t] = new_p * mask
                dst[2 * L + k, t] = new_q * mask
            return carry

        lax.fori_loop(0, L, layer_body, 0)
        for t in range(T):
            idx = jnp.concatenate([picked[j, ring(t), :] for j in range(W)], axis=1)
            chosen = jnp.zeros((8, CC), f32)
            for k in range(L):
                chosen = jnp.where(idx == k, src[k, t], chosen)
            acc[t] = acc[t] + TIME_STEP * chosen
            total = mixed[L - 1, t]
            tails = [total]
            for k in range(L - 2, -1, -1):
                total = total + mixed[k, t]
                tails.insert(0, total)
            head = None
            for k in range(L):
                term = (half * gravities[k]) * tails[k]
                head = term if head is None else head + term
                new = dst[k, t] + head
                dst[k, t, :, :COLS] = new[:, :COLS]
                dst[k, t, :, COLS:] = jnp.where(inside, new[:, COLS:], 0.0)

    def two_steps(i, carry):
        one_step(2 * i, cur, nxt)
        one_step(2 * i + 1, nxt, cur)
        return carry

    lax.fori_loop(0, N // 2, two_steps, 0)

    for t in range(T):
        for c in range(CH):
            write(COT + c, t, cur[c, t])
        write(SEA, t, acc[t])


def layer_copies(layer, picked, blocks):
    return [
        (layer.at[row : row + count, lanes(j)], picked.at[j, target : target + count, :])
        for row, target, count in blocks
        for j in range(W - 1)
    ]


def main_kernel(
    early,
    gravities_in,
    states,
    cot,
    sea,
    layer,
    spin,
    edge,
    out,
    forcing,
    planes,
    cur,
    nxt,
    mixed,
    acc,
    picked,
    flags,
    spins,
    edges,
    gravities,
    sems,
    more,
):
    @pl.when(place_of()[3] == early)
    def _():
        blocks = [(0, 0, ROWS)]
        first = start([(gravities_in, gravities), (sea, flags), (edge, edges), (spin, spins)] + layer_copies(layer, picked, blocks), more)
        copies = [own_copies(N, cot, planes, blocks, sems)]
        for n in range(N - 1, -1, -1):
            copies.append(own_copies(n, states.at[n], planes, blocks, sems))
        for group in copies:
            for copy in group:
                copy.start()
        wait(first)
        for j in range(W - 1):
            planes[SEA, j, :ROWS, :] = flags[:, lanes(j)].astype(f32)
        fill_columns(planes, edges, blocks)
        wait(copies[0])
        adjoint_steps(
            ROWS,
            lambda n: wait(own_copies(n, states.at[n], planes, blocks, sems)),
            gravities,
            spins,
            planes,
            picked,
            cur,
            nxt,
            mixed,
            acc,
        )
        pairs = []
        for j in range(W - 1):
            pairs.append((planes.at[COT : COT + CH, j, :ROWS, :], out.at[:, :, lanes(j)]))
            pairs.append((planes.at[SEA, j, :ROWS, :], forcing.at[:, lanes(j)]))
        wait(start(pairs, more))


def early_kernel(gravities, states, cot, sea, layer, spin, edge, west_in, out, forcing, west, *scratch):
    main_kernel(True, gravities, states, cot, sea, layer, spin, edge, out, forcing, *scratch)


def late_kernel(gravities, states, cot, sea, layer, spin, edge, out_in, forcing_in, out, forcing, *scratch):
    main_kernel(False, gravities, states, cot, sea, layer, spin, edge, out, forcing, *scratch)


def rim_kernel(
    gravities_in,
    own,
    sea,
    layer,
    spin,
    from_west,
    from_east,
    edge,
    out_in,
    forcing_in,
    out,
    forcing,
    fields,
    cur,
    nxt,
    mask,
    acc,
    picked,
    flags,
    layers,
    spins,
    tiles,
    gravities,
    more,
):
    first = start([(sea, flags), (layer, layers), (spin, spins), (gravities_in, gravities)], more)
    back = []
    for e, row in enumerate((0, ROWS - 8)):
        back.append((out_in.at[:, row : row + 8, :], tiles.at[e, :CH]))
        back.append((forcing_in.at[row : row + 8, :], tiles.at[e, CH]))
    back = start(back, more.at[4:])

    def put(target, at, q, e, s):
        g, k = divmod(q, 16)
        d = depth(q)
        tile = slice(0, 8) if e == 0 else slice(ROWS - 8, ROWS)
        message = (from_west, from_east)[e]
        here = 4 if e == 0 else 0
        halo = 4 - d if e == 0 else 8
        for j in range(W - 1):
            if q == SEA:
                value = flags[tile, lanes(j)].astype(f32)
            else:
                value = own[e, q // CH, q % CH, :, lanes(j)]
            target[at, j, pl.ds(8 * here + s, 8, stride=8), :] = value
            if d:
                value = message[OFFSET[q] : OFFSET[q] + d, lanes(j)]
                target[at, j, pl.ds(8 * halo + s, d, stride=8), :] = value
        shift = (124 - 8 * k) % 128
        target[at, W - 1, pl.ds(8 * here + s, 8, stride=8), :] = pltpu.roll(edge[g, tile, :], shift, 1)
        corner = pltpu.roll(message[HALO:, lanes(g)], shift, 1)
        target[at, W - 1, pl.ds(8 * (0 if e == 0 else 8) + s, 4, stride=8), :] = corner

    for e in range(2):
        for c in range(CH):
            put(cur, c // L, COT + c, e, 2 * (c % L) + e)
    wait(first)
    for e in range(2):
        for k in range(L):
            put(mask, 0, SEA, e, 2 * k + e)
            for j in range(W - 1):
                tile = slice(0, 4) if e == 0 else slice(ROWS - 4, ROWS)
                picked[j, pl.ds(2 * k + e, 4, stride=8), :] = layers[tile, lanes(j)]

    half = 0.5 * TIME_STEP
    level = lax.broadcasted_iota(jnp.int32, (8, CC), 0) // 2
    sums = []
    for k in range(L):
        sums.append(gravities[k] if k == 0 else sums[-1] + gravities[k])
    couple = []
    for m in range(L):
        weight = jnp.zeros((8, CC), f32)
        for k in range(L):
            weight = jnp.where(level == k, half * sums[min(k, (k - m) % L)], weight)
        couple.append(weight)
    keep = jnp.where(level == L - 1, 1.0 - TIME_STEP * (4.0 * VISCOSITY + BOTTOM_DRAG), 1.0 - TIME_STEP * 4.0 * VISCOSITY)
    place = place_of()
    edge_lane = lax.broadcasted_iota(jnp.int32, (8, 128), 1)
    inside = (edge_lane < 64) & place[1] | (edge_lane >= 64) & place[2]

    def row(ref, at, r):
        return jnp.concatenate([ref[at, j, pl.ds(pl.multiple_of(8 * r, 8), 8), :] for j in range(W)], axis=1)

    def set_row(ref, at, r, value):
        for j in range(W):
            ref[at, j, pl.ds(pl.multiple_of(8 * r, 8), 8), :] = value[:, lanes(j)]

    def north(x):
        return pltpu.roll(x, CC - 1, 1)

    def south(x):
        return pltpu.roll(x, 1, 1)

    for r in range(12):
        sea_r = row(mask, 0, r)
        for at in (1, 2):
            set_row(cur, at, r, row(cur, at, r) * sea_r)
    for r in range(4):
        acc[r] = jnp.zeros((8, COLS), f32)

    for i in range(N):
        n = N - 1 - i
        src, dst = (cur, nxt) if i % 2 == 0 else (nxt, cur)
        for e in range(2):
            for c in range(CH):
                put(fields, c // L, n * CH + c, e, 2 * (c % L) + e)

        for r in range(4):
            idx = jnp.concatenate([picked[j, 8 * r : 8 * r + 8, :] for j in range(W - 1)], axis=1)
            acc[r] = acc[r] + jnp.where(idx == level[:, :COLS], TIME_STEP * row(src, 0, 4 + r)[:, :COLS], 0.0)

        if n == 0:
            wait(back)
            results = []
            for e, start_row in enumerate((0, ROWS - 8)):
                for r in range(4):
                    total = acc[r]
                    total = total + pltpu.roll(total, 4, 0)
                    total = total + pltpu.roll(total, 2, 0)
                    at = r if e == 0 else 4 + r
                    tiles[e, CH, at : at + 1, :] = total[e : e + 1, :]
                results += start([(tiles.at[e, CH], forcing.at[start_row : start_row + 8, :])], more.at[2 + e :])

        def one_row(r):
            c, p, q = row(src, 0, r), row(src, 1, r), row(src, 2, r)
            h, u, v = row(fields, 0, r), row(fields, 1, r), row(fields, 2, r)
            ce, cw, cn, cs = row(src, 0, r + 1), row(src, 0, r - 1), north(c), south(c)
            pe, pw, pn, ps = row(src, 1, r + 1), row(src, 1, r - 1), north(p), south(p)
            qe, qw, qn, qs = row(src, 2, r + 1), row(src, 2, r - 1), north(q), south(q)
            ue, uw, un, us = row(fields, 1, r + 1), row(fields, 1, r - 1), north(u), south(u)
            ve, vw, vn, vs = row(fields, 2, r + 1), row(fields, 2, r - 1), north(v), south(v)
            dcx = ce - cw
            dcy = cn - cs
            mixed = (pe - pw) + (qn - qs)
            new = (1.0 - 4.0 * TIME_STEP * DIFFUSION) * c + half * (
                u * dcx + v * dcy + (2.0 * DIFFUSION) * ((ce + cw) + (cn + cs))
            )
            for m in range(L):
                new = new + couple[m] * (mixed if m == 0 else pltpu.roll(mixed, 2 * m, 0))
            new = jnp.concatenate([new[:, :COLS], jnp.where(inside, new[:, COLS:], 0.0)], axis=1)
            set_row(dst, 0, r, new)
            a_e = ue + 2.0 * VISCOSITY
            a_w = 2.0 * VISCOSITY - uw
            a_n = vn + 2.0 * VISCOSITY
            a_s = 2.0 * VISCOSITY - vs
            turn = spins[...]
            new_p = keep * p + half * (
                h * dcx
                - turn * q
                - p * (ue - uw)
                - q * (ve - vw)
                + (a_e * pe + a_w * pw)
                + (a_n * pn + a_s * ps)
            )
            new_q = keep * q + half * (
                h * dcy
                + turn * p
                - p * (un - us)
                - q * (vn - vs)
                + (a_e * qe + a_w * qw)
                + (a_n * qn + a_s * qs)
            )
            if n:
                sea_r = row(mask, 0, r)
                new_p, new_q = new_p * sea_r, new_q * sea_r
            set_row(dst, 1, r, new_p)
            set_row(dst, 2, r, new_q)

        def rows_body(b, carry):
            one_row(1 + i + 2 * b)
            one_row(2 + i + 2 * b)
            return carry

        lax.fori_loop(0, 5 - i, rows_body, 0)

    for e, start_row in enumerate((0, ROWS - 8)):
        part = slice(0, 4) if e == 0 else slice(4, 8)
        for c in range(CH):
            for j in range(W - 1):
                tiles[e, c, part, lanes(j)] = cur[c // L, j, pl.ds(32 + 2 * (c % L) + e, 4, stride=8), :]
        results += start([(tiles.at[e, :CH], out.at[:, start_row : start_row + 8, :])], more.at[e:])
    wait(results)


VMEM = pl.BlockSpec(memory_space=pltpu.VMEM)
ANY = pl.BlockSpec(memory_space=pl.ANY)
HBM = pl.BlockSpec(memory_space=pltpu.HBM)
DMA = pltpu.SemaphoreType.DMA
shape = jax.ShapeDtypeStruct


def ring_scratch(rows):
    T = rows // 8
    return [
        pltpu.VMEM((PLANES, W, rows, 128), f32),
        pltpu.VMEM((CH, T, 8, CC), f32),
        pltpu.VMEM((CH, T, 8, CC), f32),
        pltpu.VMEM((L, T, 8, CC), f32),
        pltpu.VMEM((T, 8, CC), f32),
        pltpu.VMEM((W, rows, 128), jnp.int32),
        pltpu.VMEM((ROWS, COLS), jnp.int32),
        pltpu.VMEM((8, CC), f32),
        pltpu.VMEM((GROUPS, ROWS, 128), f32),
    ]


def per_device(saved_states, final_cotangent, gravities, sea_mask, layer_index):
    lons, lats = lax.axis_size("lon"), lax.axis_size("lat")
    lat = lax.axis_index("lat")
    lane = jnp.arange(CC, dtype=jnp.int32)
    lane = jnp.where(lane < COLS + 64, lane, lane - CC)
    lat_rows = (lat * COLS + lane).astype(f32)
    spin = 2.0 * jnp.sin(jnp.pi * ((lat_rows + 0.5) / (lats * COLS) - 0.5))
    spin = jnp.broadcast_to(spin[None], (8, CC))
    strips = pl.pallas_call(
        strip_pack_kernel,
        out_shape=shape((GROUPS, ROWS, 128), f32),
        in_specs=[HBM] * 3,
        out_specs=VMEM,
        scratch_shapes=[
            pltpu.VMEM((N + 1, CH, ROWS, 128), f32),
            pltpu.VMEM((N + 1, CH, ROWS, 128), f32),
            pltpu.VMEM((ROWS, COLS), jnp.int32),
            DMA((N + 2, 2)),
        ],
        compiler_params=pltpu.CompilerParams(vmem_limit_bytes=60 << 20),
    )(saved_states, final_cotangent, sea_mask)

    def at(i, j):
        return (i % lons) * lats + j

    def swap(x, first):
        pairs = [(at(i, j), at(i, j + 1)) for i in range(lons) for j in range(first, lats - 1, 2)]
        return lax.ppermute(x, ("lon", "lat"), pairs + [(b, a) for a, b in pairs])

    def shift(x, by):
        return lax.ppermute(x, "lon", [(i, (i + by) % lons) for i in range(lons)])

    pair, middle = swap(strips, 0), swap(strips, 1)
    east, west, own = pl.pallas_call(
        row_pack_kernel,
        out_shape=[shape((MESSAGE, COLS), f32)] * 2 + [shape((2, N + 1, CH, 8, COLS), f32)],
        in_specs=[HBM] * 2,
        out_specs=[VMEM] * 3,
        scratch_shapes=[DMA((4,))],
        compiler_params=pltpu.CompilerParams(vmem_limit_bytes=51 << 20),
    )(saved_states, final_cotangent)
    edge, east, west = pl.pallas_call(
        attach_kernel,
        out_shape=[shape((GROUPS, ROWS, 128), f32)] + [shape((MESSAGE, COLS), f32)] * 2,
        in_specs=[HBM, VMEM, VMEM, HBM, HBM],
        out_specs=[VMEM, HBM, HBM],
        scratch_shapes=[pltpu.VMEM((ROWS, COLS), jnp.int32), pltpu.VMEM((2, 8, COLS), f32), DMA((2,))],
        input_output_aliases={3: 1, 4: 2},
        compiler_params=pltpu.CompilerParams(vmem_limit_bytes=51 << 20),
    )(sea_mask, pair, middle, east, west)

    outs = [shape((CH, ROWS, COLS), f32), shape((ROWS, COLS), f32)]
    main = dict(
        scratch_shapes=ring_scratch(ROWS) + [pltpu.SMEM((L,), f32), DMA((N + 1, W - 1, 1)), DMA((16,))],
        compiler_params=pltpu.CompilerParams(vmem_limit_bytes=51 << 20),
        cost_estimate=pl.CostEstimate(flops=160_000_000, bytes_accessed=24_000_000, transcendentals=0),
    )
    fixed = (gravities, saved_states, final_cotangent, sea_mask, layer_index, spin, edge)
    specs = [ANY] + [HBM] * 4 + [ANY] * 2
    from_west = shift(east, 1)
    out, forcing, west = pl.pallas_call(
        early_kernel,
        out_shape=outs + [shape((MESSAGE, COLS), f32)],
        in_specs=specs + [HBM],
        out_specs=[HBM] * 3,
        input_output_aliases={7: 2},
        **main,
    )(*fixed, west)
    from_east = shift(west, -1)
    out, forcing = pl.pallas_call(
        late_kernel,
        out_shape=outs,
        in_specs=specs + [HBM] * 2,
        out_specs=[HBM] * 2,
        input_output_aliases={7: 0, 8: 1},
        **main,
    )(*fixed, out, forcing)

    return pl.pallas_call(
        rim_kernel,
        out_shape=outs,
        in_specs=[ANY, VMEM, ANY, ANY, ANY] + [VMEM] * 3 + [HBM] * 2,
        out_specs=[HBM, HBM],
        scratch_shapes=[
            pltpu.VMEM((3, W, 96, 128), f32),
            pltpu.VMEM((3, W, 96, 128), f32),
            pltpu.VMEM((3, W, 96, 128), f32),
            pltpu.VMEM((1, W, 96, 128), f32),
            pltpu.VMEM((4, 8, COLS), f32),
            pltpu.VMEM((W - 1, 32, 128), jnp.int32),
            pltpu.VMEM((ROWS, COLS), jnp.int32),
            pltpu.VMEM((ROWS, COLS), jnp.int32),
            pltpu.VMEM((8, CC), f32),
            pltpu.VMEM((2, CH + 1, 8, COLS), f32),
            pltpu.SMEM((L,), f32),
            DMA((8,)),
        ],
        input_output_aliases={8: 0, 9: 1},
        compiler_params=pltpu.CompilerParams(vmem_limit_bytes=51 << 20),
    )(
        gravities,
        own,
        sea_mask,
        layer_index,
        spin,
        from_west,
        from_east,
        edge,
        out,
        forcing,
    )


def solution(mesh):
    return jax.shard_map(
        per_device,
        mesh=mesh,
        in_specs=(
            P(None, None, "lon", "lat"),
            P(None, "lon", "lat"),
            P(),
            P("lon", "lat"),
            P("lon", "lat"),
        ),
        out_specs=(P(None, "lon", "lat"), P("lon", "lat")),
        check_vma=False,
    )
```
